128 devices in a mesh: gy: 8 (over x, core), gz: 16 (over z, y).
Axes of the slice: x: 4, y: 4, z: 4, core: 2. Of those that a mesh axis runs over, the one named last changes fastest.
Arguments:
- features: bfloat16 [64, 64, 32, 512], P('gy', 'gz'), may hold values from -6 to 6
- cotangent: bfloat16 [64, 64, 32, 512], P('gy', 'gz'), may hold values from -6 to 6
- spectral_weight: bfloat16 [32, 32, 65536], P('gz', None, 'gy'), may hold values from -6 to 6
- kernel_weight: bfloat16 [3, 3, 32, 96], replicated, may hold values from -0.21875 to 0.21875
- channel_bias: float32 [32], replicated, may hold values from -4 to 4
Outputs:
- grad_field: bfloat16 [64, 64, 32, 512], P('gy', 'gz')
- grad_spectral: float32 [32, 32, 65536], P('gz', None, 'gy')
- grad_kernel: float32 [3, 3, 32, 96], replicated
- grad_bias: float32 [32], replicated
The draws below stay inside these ranges and needn't reach their ends.
All inputs are finite; a program needn't handle non-finite values.
Results may differ from the reference program's by a relative error of at most 0.0075.
Values may be sent and summed in bfloat16 or wider, within the bound.
No kernel may reach another device: no remote copies, remote signals or barrier semaphores. Data moves between devices by JAX's collectives and lax.ppermute only.
A program may use at most 192 MiB of HBM per device.

```python
import math
import jax
import jax.numpy as jnp
from jax import lax

NX = 512
C = 32
MX = 32
MY = 32
MZ = 32
NY = 64
NZ = 64


def shard_levels(stream_key, dims, split, least, largest):
    def one(position, shards_of):
        draws = jax.random.uniform(jax.random.fold_in(jax.random.fold_in(stream_key, 6), position), (shards_of,), jnp.float32, least / len(split), largest / len(split))
        return jnp.repeat(jnp.exp(draws), dims[position] // shards_of).reshape((-1,) + (1,) * (len(dims) - position - 1))

    level = one(*split[0])
    for cut in split[1:]:
        level = level * one(*cut)
    return level


def gaussian(key, dims, spread, bound, shards=(), kind=jnp.bfloat16):
    drawn = spread * jax.random.normal(key, dims, jnp.float32)
    if shards:
        drawn = drawn * shard_levels(key, dims, shards, -0.22, 0.18)
    return jnp.clip(drawn, -bound, bound).astype(kind)


def setup_inputs(seed: int = 0) -> dict:
    key_list = jax.random.split(jax.random.key(seed), 6)
    features = gaussian(key_list[0], (NY, NZ, C, NX), 1.0, 6.0, ((0, 8), (1, 16)))
    cotangent = gaussian(key_list[1], (NY, NZ, C, NX), 1.0, 6.0, ((0, 8), (1, 16)))
    spectral_weight = gaussian(key_list[2], (MY, MZ, MX * 2 * C * C), 1.0, 6.0, ((0, 16), (2, 8)))
    kernel_weight = gaussian(key_list[3], (3, 3, C, 3 * C), (27 * C) ** -0.5, 0.21875)
    channel_bias = gaussian(key_list[4], (C,), 1.0, 4.0, (), jnp.float32)
    return dict(features=features, cotangent=cotangent, spectral_weight=spectral_weight, kernel_weight=kernel_weight, channel_bias=channel_bias)


def mode_freqs(positions, modes_kept, length):
    return jnp.where(positions < modes_kept // 2, positions, length - modes_kept + positions).astype(jnp.int32)

def phase_table(out_places, sum_places, length, rotation):
    products = out_places[:, None] * sum_places[None, :] % length
    angles = 2.0 * math.pi / length * products.astype(jnp.float32)
    cosine = jnp.cos(angles)
    sine_part = rotation * jnp.sin(angles)
    row_real = jnp.stack([cosine, -sine_part], axis=-1)
    row_imag = jnp.stack([sine_part, cosine], axis=-1)
    return jnp.stack([row_real, row_imag], axis=1)

def grid_table(length, modes_kept):
    places = jnp.arange(length, dtype=jnp.int32)
    frequency = jnp.arange(modes_kept, dtype=jnp.int32)
    products = places[:, None] * frequency[None, :] % length
    angles = 2.0 * math.pi / length * products.astype(jnp.float32)
    return jnp.stack([jnp.cos(angles), -jnp.sin(angles)], axis=-1)

def line_forward(block, modes_kept, norm_scale):
    rows_here, depth_here, channels, length = block.shape
    lookup = grid_table(length, modes_kept).reshape(length, 2 * modes_kept).astype(jnp.bfloat16)
    projected = jnp.dot(block.reshape(-1, length), lookup, preferred_element_type=jnp.float32)
    projected = projected.reshape(rows_here, depth_here, channels, modes_kept, 2).transpose(0, 1, 3, 4, 2)
    return (norm_scale * projected).reshape(rows_here, depth_here, modes_kept * 2 * channels)

def line_inverse(spectrum, channels, length, norm_scale):
    rows_here, depth_here, merged = spectrum.shape
    modes_kept = merged // (2 * channels)
    lookup = grid_table(length, modes_kept).transpose(1, 2, 0)
    pieces = spectrum.reshape(rows_here, depth_here, modes_kept, 2, channels)
    return norm_scale * jnp.einsum('yzmpc,mpx->yzcx', pieces, lookup, precision=lax.Precision.HIGHEST)

def along_first(lookup, values, channels):
    first_len, second_len, merged = values.shape
    pieces = values.reshape(first_len, second_len, merged // (2 * channels), 2, channels)
    result = jnp.einsum('kqap,abmpc->kbmqc', lookup, pieces, precision=lax.Precision.HIGHEST)
    return result.reshape(lookup.shape[0], second_len, merged)

def along_second(lookup, values, channels):
    first_len, second_len, merged = values.shape
    pieces = values.reshape(first_len, second_len, merged // (2 * channels), 2, channels)
    result = jnp.einsum('kqbp,abmpc->akmqc', lookup, pieces, precision=lax.Precision.HIGHEST)
    return result.reshape(first_len, lookup.shape[0], merged)

def split_parts(spectrum, channels):
    first_len, second_len, merged = spectrum.shape
    pieces = spectrum.reshape(first_len, second_len, merged // (2 * channels), 2, channels)
    return (pieces[:, :, :, 0], pieces[:, :, :, 1])

def split_weight(weight, channels):
    first_len, second_len, merged = weight.shape
    pieces = weight.astype(jnp.float32).reshape(first_len, second_len, merged // (2 * channels * channels), 2, channels, channels)
    return (pieces[:, :, :, 0], pieces[:, :, :, 1])

def mix_modes(spectrum, weight, mode_gain, channels):
    real_in, imag_in = split_parts(spectrum, channels)
    real_w, imag_w = split_weight(weight, channels)
    contract = lambda left, right: jnp.einsum('abmc,abmco->abmo', left, right, precision=lax.Precision.HIGHEST)
    real_out = contract(real_in, real_w) - contract(imag_in, imag_w)
    imag_out = contract(real_in, imag_w) + contract(imag_in, real_w)
    stacked = jnp.stack([real_out, imag_out], axis=3) * mode_gain[None, None, :, None, None]
    return stacked.reshape(spectrum.shape)

def mix_adjoint(spectrum, back_spectrum, weight, mode_gain, channels):
    real_in, imag_in = split_parts(spectrum, channels)
    real_back, imag_back = split_parts(back_spectrum, channels)
    real_w, imag_w = split_weight(weight, channels)
    to_input = lambda left, right: jnp.einsum('abmo,abmco->abmc', left, right, precision=lax.Precision.HIGHEST)
    outer_prod = lambda left, right: jnp.einsum('abmc,abmo->abmco', left, right, precision=lax.Precision.HIGHEST)
    gain_modes = mode_gain[None, None, :, None, None]
    real_mode = to_input(real_back, real_w) + to_input(imag_back, imag_w)
    imag_mode = to_input(imag_back, real_w) - to_input(real_back, imag_w)
    grad_modes = (jnp.stack([real_mode, imag_mode], axis=3) * gain_modes).reshape(spectrum.shape)
    real_grad = outer_prod(real_in, real_back) + outer_prod(imag_in, imag_back)
    imag_grad = outer_prod(real_in, imag_back) - outer_prod(imag_in, real_back)
    gain_weight = mode_gain[None, None, :, None, None, None]
    grad_weight = jnp.stack([real_grad, imag_grad], axis=3) * gain_weight
    return (grad_modes, grad_weight.reshape(weight.shape))

def conv_local(values, kernel):
    rhs_kernel = kernel.reshape(3, 3, C, 3, C)
    result = lax.conv_general_dilated(values[None], rhs_kernel, (1, 1, 1), 'SAME', dimension_numbers=('NHDCW', 'HDOWI', 'NHDCW'), precision=lax.Precision.HIGHEST)
    return result[0]

def analyse(block, norm_scale):
    spectrum = line_forward(block, MX, norm_scale)
    freq_y = mode_freqs(jnp.arange(MY, dtype=jnp.int32), MY, NY)
    freq_z = mode_freqs(jnp.arange(MZ, dtype=jnp.int32), MZ, NZ)
    spectrum = along_first(phase_table(freq_y, jnp.arange(NY, dtype=jnp.int32), NY, -1.0), spectrum, C)
    return along_second(phase_table(freq_z, jnp.arange(NZ, dtype=jnp.int32), NZ, -1.0), spectrum, C)

def synthesize(spectrum, norm_scale):
    freq_y = mode_freqs(jnp.arange(MY, dtype=jnp.int32), MY, NY)
    freq_z = mode_freqs(jnp.arange(MZ, dtype=jnp.int32), MZ, NZ)
    spectrum = along_second(phase_table(jnp.arange(NZ, dtype=jnp.int32), freq_z, NZ, 1.0), spectrum, C)
    spectrum = along_first(phase_table(jnp.arange(NY, dtype=jnp.int32), freq_y, NY, 1.0), spectrum, C)
    return line_inverse(spectrum, C, NX, norm_scale)

def reference(features, cotangent, spectral_weight, kernel_weight, channel_bias):
    norm_scale = 1.0 / math.sqrt(NX * NY * NZ)
    mode_gain = jnp.where(jnp.arange(MX) == 0, 1.0, 2.0).astype(jnp.float32)
    spectrum = analyse(features, norm_scale)
    spectral = synthesize(mix_modes(spectrum, spectral_weight, mode_gain, C), norm_scale)
    local, conv_pull = jax.vjp(conv_local, features.astype(jnp.float32), kernel_weight.astype(jnp.float32))
    pre = spectral + local + channel_bias[None, None, :, None]
    _, gelu_pull = jax.vjp(jax.nn.gelu, pre)
    slope, = gelu_pull(cotangent.astype(jnp.float32))
    slope = slope.astype(jnp.bfloat16)
    back_spectrum = analyse(slope, norm_scale)
    grad_modes, grad_spectral = mix_adjoint(spectrum, back_spectrum, spectral_weight, mode_gain, C)
    back_field = synthesize(grad_modes, norm_scale)
    conv_field, conv_kernel = conv_pull(slope.astype(jnp.float32))
    grad_field = (back_field + conv_field).astype(jnp.bfloat16)
    grad_kernel = norm_scale * conv_kernel.reshape(3, 3, C, 3 * C)
    grad_bias = norm_scale * lax.optimization_barrier(jnp.sum(slope.astype(jnp.float32), axis=(0, 1, 3)))
    return (grad_field, grad_spectral, grad_kernel, grad_bias)
```

```python
import functools
import math

import jax
import jax.numpy as jnp
import ml_dtypes
import numpy as np
from jax import lax
from jax.experimental import pallas as pl
from jax.experimental.pallas import tpu as pltpu
from jax.sharding import PartitionSpec as P

NX, NY, NZ = 512, 64, 64
C = 32
GY, GZ = 8, 16
YL, ZL = 8, 4
KXL = 4
ROWS = 24
SCALE = 1.0 / math.sqrt(NX * NY * NZ)
F32, BF16 = jnp.float32, jnp.bfloat16
VMEM_BYTES = 32 * 1024 * 1024


def freqs(count, length):
    index = np.arange(count)
    return np.where(index < count // 2, index, length - count + index)


def angle(a, b, length):
    return 2.0 * math.pi / length * ((a[:, None] * b[None, :]) % length)


def split_np(table):
    high = table.astype(ml_dtypes.bfloat16)
    low = (table - high.astype(np.float64)).astype(ml_dtypes.bfloat16)
    return high, low


def x_forward_table():
    turn = angle(np.arange(32), np.arange(NX), NX)
    both = np.stack([np.cos(turn), -np.sin(turn)], 0).reshape(2, GY, KXL, NX)
    return both.transpose(1, 0, 2, 3).reshape(64, NX).astype(ml_dtypes.bfloat16)


def x_inverse_table():
    turn = angle(np.arange(32), np.arange(NX), NX)
    both = np.stack([np.cos(turn), -np.sin(turn)], 1).reshape(64, NX)
    high, low = split_np(both)
    return np.concatenate([high, low, high], 0)


def rotation(turn, sign):
    cos, sin = np.cos(turn), sign * np.sin(turn)
    return np.stack([np.stack([cos, -sin], -1), np.stack([sin, cos], -1)], 1)


def y_forward_tables():
    every = []
    for g in range(GY):
        turn = angle(freqs(32, NY), g * YL + np.arange(YL), NY)
        table = rotation(turn, -1.0).reshape(GZ, 2, 2, YL, 2)
        full = np.einsum("gkpyq,ab->gakpyqb", table, np.eye(KXL)).reshape(256, 64)
        high, low = split_np(full)
        every.append(np.concatenate([high, low, high], 1))
    return np.stack(every)


def z_forward_table():
    turn = angle(freqs(32, NZ), np.arange(NZ), NZ)
    table = SCALE * rotation(turn, -1.0).reshape(32, 2, GZ, ZL, 2)
    full = np.einsum("kpgzq,ab->pakzbqg", table, np.eye(2)).reshape(128, 256)
    return np.stack(split_np(full))


def z_inverse_table():
    turn = angle(np.arange(NZ), freqs(32, NZ), NZ)
    table = SCALE * rotation(turn, 1.0).reshape(GZ, ZL, 2, 32, 2)
    full = np.einsum("gzpkq,ab->gapzqbk", table, np.eye(2)).reshape(256, 128)
    return np.stack(split_np(full))


def y_inverse_tables():
    every = []
    for g in range(GY):
        turn = angle(g * YL + np.arange(YL), freqs(32, NY), NY)
        table = rotation(turn, 1.0).reshape(YL, 2, GZ, 2, 2)
        full = np.einsum("ypgkq,ab->apygkqb", table, np.eye(ZL)).reshape(64, 256)
        every.append(np.concatenate(split_np(full), 0))
    return np.stack(every)


def split(value):
    high = value.astype(BF16)
    return high, (value - high.astype(F32)).astype(BF16)


def dot(a, b):
    return jnp.dot(a, b, preferred_element_type=F32)


def dot_nt(a, b):
    return lax.dot_general(a, b, (((1,), (1,)), ((), ())), preferred_element_type=F32)


def dot_tn(a, b):
    return lax.dot_general(a, b, (((0,), (0,)), ((), ())), preferred_element_type=F32)


def lane_of(shape):
    return lax.broadcasted_iota(jnp.int32, shape, len(shape) - 1)


def swap_blocks(parts):
    lane = lane_of(parts[0].shape)
    half = lane < 64
    p0, p1, p2, p3 = parts
    q0 = jnp.where(half, p0, pltpu.roll(p2, 64, 1))
    q2 = jnp.where(half, pltpu.roll(p0, 64, 1), p2)
    q1 = jnp.where(half, p1, pltpu.roll(p3, 64, 1))
    q3 = jnp.where(half, pltpu.roll(p1, 64, 1), p3)
    even = (lane & 32) == 0
    out = []
    for lo, hi in ((q0, q1), (q2, q3)):
        out.append(jnp.where(even, lo, pltpu.roll(hi, 32, 1)))
        out.append(jnp.where(even, pltpu.roll(lo, 96, 1), hi))
    return out


def y_forward(lines, table):
    blocks = []
    for g in range(GY):
        blocks.append(jnp.concatenate([line[g * 8 : g * 8 + 8] for line in lines], 0))
    joined = jnp.concatenate(blocks, 1)
    high, low = split(joined)
    return dot(table, jnp.concatenate([high, high, low], 0))


def collect_spectrum(recv_ref, table_ref, sums_ref):
    total = recv_ref[0:GZ, 0:16, :].astype(F32)
    for g in range(1, GY):
        total = total + recv_ref[g * GZ : (g + 1) * GZ, 0:16, :].astype(F32)
    sums_ref[...] = total.reshape(256, 128)
    turned = []
    for j in range(4):
        turned.append(
            swap_blocks([sums_ref[pl.ds(k * 4 + j, GZ, stride=16), :] for k in range(KXL)])
        )
    joined = jnp.concatenate([turned[j][z] for z in range(ZL) for j in range(4)], 0)
    high, low = split(joined)
    return dot(table_ref[0], high) + dot(table_ref[1], high) + dot(table_ref[0], low)


def z_inverse(modes, table_ref):
    high, low = split(modes)
    return dot(table_ref[0], high) + dot(table_ref[1], high) + dot(table_ref[0], low)


def gain_lanes():
    lane = lane_of((128, 128))
    first = jnp.logical_and(lane < 32, lax.axis_index("gy") == 0)
    return jnp.where(first, 1.0, 2.0).astype(F32)


def repeat_matrix():
    row = lax.broadcasted_iota(jnp.int32, (64, 1024), 0) & 31
    return jnp.where(row == lane_of((64, 1024)) // 32, 1.0, 0.0).astype(BF16)


def spread(spectrum, k, matrix):
    high, low = split(spectrum[:, k * 32 : k * 32 + 32])
    return dot(jnp.concatenate([high, low], 1), matrix)


def fold_tiles(value):
    total = value[:, 0:128]
    for t in range(1, 8):
        total = total + value[:, t * 128 : t * 128 + 128]
    total = total + pltpu.roll(total, 64, 1)
    return total + pltpu.roll(total, 32, 1)


def synth_fields(recv_ref, table, field_ref):
    joined = jnp.concatenate(
        [recv_ref[g * GZ : (g + 1) * GZ, 0:16, :].reshape(256, 128) for g in range(GY)], 1
    )
    both = dot(table, joined)
    planes = both[0:64] + both[64:128]
    for g in range(GY):
        cols = planes[:, g * 128 : g * 128 + 128]
        turned = swap_blocks([cols[z * 16 : z * 16 + 16] for z in range(ZL)])
        for k in range(KXL):
            for part in range(2):
                field_ref[pl.ds((g * 4 + k) * 2 + part, YL, stride=64), :] = turned[k][
                    part * 8 : part * 8 + 8
                ]


def x_inverse(field, table):
    high, low = split(field)
    return dot_tn(jnp.concatenate([high, high, low], 0), table)


def shift_right(value):
    return jnp.where(lane_of(value.shape) == 0, 0.0, pltpu.roll(value, 1, 1))


def shift_left(value):
    return jnp.where(lane_of(value.shape) == NX - 1, 0.0, pltpu.roll(value, NX - 1, 1))


def analyse_kernel(idx_ref, field_ref, tx_ref, ty_ref, send_ref):
    lines = [dot_nt(tx_ref[...], field_ref[y]) for y in range(YL)]
    out = y_forward(lines, ty_ref[0])
    for g in range(GY):
        block = out[:, g * 128 : g * 128 + 128].astype(BF16)
        send_ref[g * GZ : (g + 1) * GZ] = block.reshape(GZ, 16, 128)


def mix_kernel(recv_ref, weight_ref, tzf_ref, tzi_ref, send_ref, spec_ref, sums_ref):
    spectrum = collect_spectrum(recv_ref, tzf_ref, sums_ref)
    spec_ref[...] = spectrum
    matrix = repeat_matrix()
    lane = lane_of((64, 128)) // 32
    real = jnp.zeros((64, 128), F32)
    imag = jnp.zeros((64, 128), F32)
    for k in range(KXL):
        wide = spread(spectrum, k, matrix)
        w_re = weight_ref[:, k * 2048 : k * 2048 + 1024].astype(F32)
        w_im = weight_ref[:, k * 2048 + 1024 : k * 2048 + 2048].astype(F32)
        s_re, s_im = wide[0:64], wide[64:128]
        real = jnp.where(lane == k, fold_tiles(s_re * w_re - s_im * w_im), real)
        imag = jnp.where(lane == k, fold_tiles(s_re * w_im + s_im * w_re), imag)
    modes = jnp.concatenate([real, imag], 0) * gain_lanes()
    block = z_inverse(modes, tzi_ref).astype(BF16).reshape(GZ, 16, 128)
    for g in range(GY):
        send_ref[g * GZ : (g + 1) * GZ] = block


def conv_rows(pad_ref, taps_ref, y):
    window = pad_ref[pl.ds(y, 3)].reshape(576, NX)
    wide = dot(taps_ref[...], window)
    return wide[128:256] + shift_right(wide[0:128]) + shift_left(wide[256:384])


def build_taps(kernel_ref, taps_ref):
    zero = jnp.zeros((C, C), F32)
    for dx in range(3):
        for z in range(ZL):
            parts = []
            for dy in range(3):
                for zin in range(ZL + 2):
                    dz = zin - z
                    if 0 <= dz < 3:
                        parts.append(
                            kernel_ref[dy, dz].astype(F32)[:, dx * C : dx * C + C]
                        )
                    else:
                        parts.append(zero)
            row = (dx * ZL + z) * C
            taps_ref[row : row + C, :] = jnp.concatenate(parts, 1).astype(BF16)


def fill_pad(pad_ref, own_ref, ylo_ref, yhi_ref, zlo_ref, zhi_ref):
    pad_ref[:, 0:32] = zlo_ref[...]
    pad_ref[:, 160:192] = zhi_ref[...]
    pad_ref[1:9, 32:160] = own_ref[...]
    pad_ref[0, 32:160] = ylo_ref[...]
    pad_ref[9, 32:160] = yhi_ref[...]


def conv_kernel(own_ref, ylo_ref, yhi_ref, zlo_ref, zhi_ref, kernel_ref, bias_ref, out_ref, pad_ref, taps_ref):
    fill_pad(pad_ref, own_ref, ylo_ref, yhi_ref, zlo_ref, zhi_ref)
    build_taps(kernel_ref, taps_ref)

    def step(y, carry):
        out_ref[y] = conv_rows(pad_ref, taps_ref, y) + bias_ref[...]
        return carry

    lax.fori_loop(0, YL, step, 0)


def slope_kernel(
    idx_ref, recv_ref, local_ref, cot_ref, pad_ref, tyi_ref, txi_ref, tx_ref, ty_ref,
    slope_ref, send_ref, field_ref, sums_ref, rows_ref,
):
    synth_fields(recv_ref, tyi_ref[0], field_ref)
    root = math.sqrt(2.0 / math.pi)
    sums_ref[...] = jnp.zeros_like(sums_ref)
    lines = []
    bias = jnp.zeros((128, 1), F32)
    for y in range(YL):
        pre = x_inverse(field_ref[y * 64 : y * 64 + 64], txi_ref[...]) + local_ref[y]
        square = pre * pre
        bent = jnp.tanh(root * pre * (1.0 + 0.044715 * square))
        rate = 0.5 * (1.0 + bent) + 0.5 * root * pre * (1.0 - bent * bent) * (
            1.0 + 3.0 * 0.044715 * square
        )
        slope = (cot_ref[y].astype(F32) * rate).astype(BF16)
        slope_ref[y] = slope
        lines.append(dot_nt(tx_ref[...], slope))
        wide = slope.astype(F32)
        bias = bias + jnp.sum(wide, axis=1, keepdims=True)
        three = jnp.concatenate(
            [shift_left(wide).astype(BF16), slope, shift_right(wide).astype(BF16)], 0
        )
        sums_ref[...] += dot_nt(three, pad_ref[y : y + 3].reshape(576, NX))
    out = y_forward(lines, ty_ref[0])
    for g in range(GY):
        block = out[:, g * 128 : g * 128 + 128].astype(BF16)
        send_ref[g * GZ : (g + 1) * GZ, 0:16] = block.reshape(GZ, 16, 128)
    bias32 = bias[0:32] + bias[32:64] + bias[64:96] + bias[96:128]
    lane = lane_of((C, 128))
    rows_ref[...] = jnp.zeros_like(rows_ref)
    for dx in range(3):
        for dy in range(3):
            total = jnp.zeros((C, 96), F32)
            for z in range(ZL):
                row = (dx * ZL + z) * C
                col = dy * 192 + z * C
                total = total + sums_ref[row : row + C, col : col + 96]
            total = jnp.concatenate([total, jnp.zeros((C, 32), F32)], 1)
            total = jnp.where(lane == 96, bias32, total)
            high = total.astype(BF16).astype(F32)
            rows_ref[pl.ds(dx * C * 8 + dy, C, stride=8), :] = high
            rows_ref[pl.ds(dx * C * 8 + dy + 3, C, stride=8), :] = total - high
    send_ref[:, 16:24] = rows_ref[...].reshape(128, 8, 128).astype(BF16)


def adjoint_kernel(recv_ref, weight_ref, tzf_ref, tzi_ref, send_ref, spec_ref, sums_ref):
    spectrum = collect_spectrum(recv_ref, tzf_ref, sums_ref)
    spec_ref[...] = spectrum
    row = lax.broadcasted_iota(jnp.int32, (1024, 128), 0) // 32
    lane = lane_of((1024, 128))
    gather = []
    for k in range(KXL):
        w_re = weight_ref[:, k * 2048 : k * 2048 + 1024].astype(F32)
        w_im = weight_ref[:, k * 2048 + 1024 : k * 2048 + 2048].astype(F32)
        own = spectrum[:, k * 32 : k * 32 + 32]
        four = jnp.concatenate([own] * 4, 1)
        wide = jnp.concatenate([four] * 8, 1)
        b_re, b_im = wide[0:64], wide[64:128]
        both = jnp.concatenate([b_re * w_re + b_im * w_im, b_im * w_re - b_re * w_im], 0)
        matrix = jnp.where(row + k * 32 == lane, 1.0, 0.0).astype(BF16)
        high, low = split(both)
        gather.append(dot(high, matrix) + dot(low, matrix))
    modes = (gather[0] + gather[1] + gather[2] + gather[3]) * gain_lanes()
    block = z_inverse(modes, tzi_ref).astype(BF16).reshape(GZ, 16, 128)
    total = jnp.sum(recv_ref[:, 16:24].astype(F32), axis=0)
    total = total + pltpu.roll(total, 5, 0)
    high = total.astype(BF16).astype(F32)
    low = total - high
    part = lax.broadcasted_iota(jnp.int32, (8, 128), 0)
    tail = jnp.where(part < 3, high, jnp.where(part < 6, pltpu.roll(low, 3, 0), 0.0)).astype(BF16)
    tail = jnp.broadcast_to(tail[None], (GZ, 8, 128))
    for g in range(GY):
        send_ref[g * GZ : (g + 1) * GZ, 0:16] = block
        send_ref[g * GZ : (g + 1) * GZ, 16:24] = tail


def outer_kernel(spec_ref, back_ref, out_ref):
    matrix = repeat_matrix()
    gain = gain_lanes()
    spectrum = spec_ref[...]
    back = back_ref[...] * gain
    for k in range(KXL):
        wide = spread(spectrum, k, matrix)
        s_re, s_im = wide[0:64], wide[64:128]
        own = back[:, k * 32 : k * 32 + 32]
        four = jnp.concatenate([own] * 4, 1)
        tiled = jnp.concatenate([four] * 8, 1)
        b_re, b_im = tiled[0:64], tiled[64:128]
        out_ref[:, k * 2048 : k * 2048 + 1024] = s_re * b_re + s_im * b_im
        out_ref[:, k * 2048 + 1024 : k * 2048 + 2048] = s_re * b_im - s_im * b_re


def final_kernel(
    idx_ref, recv_ref, conv_ref, tyi_ref, txi_ref, grad_ref, kernel_ref, bias_ref, field_ref, rows_ref
):
    synth_fields(recv_ref, tyi_ref[0], field_ref)
    for y in range(YL):
        back = x_inverse(field_ref[y * 64 : y * 64 + 64], txi_ref[...])
        grad_ref[y] = (back + conv_ref[y]).astype(BF16)
    rows_ref[...] = recv_ref[:, 16:24].astype(F32).reshape(1024, 128)
    for dy in range(3):
        three = []
        for dx in range(3):
            high = rows_ref[pl.ds(dx * C * 8 + dy, C, stride=8), :]
            low = rows_ref[pl.ds(dx * C * 8 + dy + 3, C, stride=8), :]
            three.append(SCALE * (high + low))
        for dz in range(3):
            kernel_ref[dy, dz] = jnp.concatenate([t[:, dz * C : dz * C + C] for t in three], 1)
        if dy == 0:
            bias_ref[...] = three[0][:, 96:97]


def call(body, out_shape, scratch=(), flops=0, nbytes=0, **extra):
    return pl.pallas_call(
        body,
        out_shape=out_shape,
        scratch_shapes=list(scratch),
        compiler_params=pltpu.CompilerParams(vmem_limit_bytes=VMEM_BYTES),
        cost_estimate=pl.CostEstimate(flops=flops, bytes_accessed=nbytes, transcendentals=0),
        **extra,
    )


def call_indexed(body, operands, out_shape, by_index, scratch=(), flops=0, nbytes=0):
    def whole(shape):
        return pl.BlockSpec(shape, lambda i, idx, n=len(shape): (0,) * n)

    def mine(shape):
        return pl.BlockSpec((1,) + shape[1:], lambda i, idx, n=len(shape): (idx[0],) + (0,) * (n - 1))

    in_specs = [
        mine(a.shape) if n in by_index else whole(a.shape) for n, a in enumerate(operands)
    ]
    shapes = out_shape if isinstance(out_shape, (tuple, list)) else (out_shape,)
    out_specs = [whole(s.shape) for s in shapes]
    if not isinstance(out_shape, (tuple, list)):
        out_specs = out_specs[0]
    index = lax.axis_index("gy").astype(jnp.int32).reshape(1)
    return pl.pallas_call(
        body,
        out_shape=out_shape,
        grid_spec=pltpu.PrefetchScalarGridSpec(
            num_scalar_prefetch=1,
            grid=(1,),
            in_specs=in_specs,
            out_specs=out_specs,
            scratch_shapes=list(scratch),
        ),
        compiler_params=pltpu.CompilerParams(vmem_limit_bytes=VMEM_BYTES),
        cost_estimate=pl.CostEstimate(flops=flops, bytes_accessed=nbytes, transcendentals=0),
    )(index, *operands)


def exchange(blocks):
    return lax.all_to_all(blocks, ("gy", "gz"), 0, 0, tiled=True)


def halos(own):
    up = [(i, i + 1) for i in range(GY - 1)]
    down = [(i + 1, i) for i in range(GY - 1)]
    ylo = lax.ppermute(own[YL - 1], "gy", up)
    yhi = lax.ppermute(own[0], "gy", down)
    ahead = [(i, i + 1) for i in range(GZ - 1)]
    behind = [(i + 1, i) for i in range(GZ - 1)]
    last = jnp.concatenate([ylo[None, 96:128], own[:, 96:128], yhi[None, 96:128]], 0)
    first = jnp.concatenate([ylo[None, 0:32], own[:, 0:32], yhi[None, 0:32]], 0)
    zlo = lax.ppermute(last, "gz", ahead)
    zhi = lax.ppermute(first, "gz", behind)
    return ylo, yhi, zlo, zhi


def shape(dims, kind):
    return jax.ShapeDtypeStruct(dims, kind)


def conv(own, halo, kernel, bias):
    return call(
        conv_kernel,
        (shape((YL, 128, NX), F32), shape((YL + 2, 192, NX), BF16)),
        [pltpu.VMEM((384, 576), BF16)],
        flops=2 * YL * 384 * 576 * NX,
        nbytes=6 << 20,
    )(own, *halo, kernel, bias)


def on_device(features, cotangent, spectral_weight, kernel_weight, channel_bias):
    own = features.reshape(YL, 128, NX)
    cot = cotangent.reshape(YL, 128, NX)
    weight = spectral_weight.reshape(64, 8192)
    tx = jnp.asarray(x_forward_table())
    txi = jnp.asarray(x_inverse_table())
    ty = jnp.asarray(y_forward_tables())
    tyi = jnp.asarray(y_inverse_tables())
    tzf = jnp.asarray(z_forward_table())
    tzi = jnp.asarray(z_inverse_table())
    bias_rows = jnp.tile(channel_bias, ZL).reshape(128, 1)
    flipped = kernel_weight.reshape(3, 3, C, 3, C)[::-1, ::-1, :, ::-1, :]
    flipped = flipped.transpose(0, 1, 4, 3, 2).reshape(3, 3, C, 3 * C)

    send = call_indexed(
        analyse_kernel, (own, tx, ty), shape((128, 16, 128), BF16), (2,), flops=1 << 27, nbytes=2 << 20
    )
    recv = exchange(send)
    halo = halos(own)
    local, padded = conv(own, halo, kernel_weight, bias_rows)
    send, spectrum = call(
        mix_kernel,
        (shape((128, 16, 128), BF16), shape((128, 128), F32)),
        [pltpu.VMEM((256, 128), F32)],
        flops=1 << 27,
        nbytes=2 << 20,
    )(recv, weight, tzf, tzi)
    recv = exchange(send)
    slope, send = call_indexed(
        slope_kernel,
        (recv, local, cot, padded, tyi, txi, tx, ty),
        (shape((YL, 128, NX), BF16), shape((128, ROWS, 128), BF16)),
        (4, 7),
        [
            pltpu.VMEM((512, 128), F32),
            pltpu.VMEM((384, 576), F32),
            pltpu.VMEM((1024, 128), F32),
        ],
        flops=1 << 31,
        nbytes=8 << 20,
    )
    recv = exchange(send)
    halo = halos(slope)
    conv_field, _ = conv(slope, halo, flipped, jnp.zeros((128, 1), F32))
    send, back = call(
        adjoint_kernel,
        (shape((128, ROWS, 128), BF16), shape((128, 128), F32)),
        [pltpu.VMEM((256, 128), F32)],
        flops=1 << 27,
        nbytes=2 << 20,
    )(recv, weight, tzf, tzi)
    recv = exchange(send)
    grad_spectral = call(
        outer_kernel, shape((64, 8192), F32), flops=1 << 27, nbytes=3 << 20
    )(spectrum, back)
    grad_field, grad_kernel, grad_bias = call_indexed(
        final_kernel,
        (recv, conv_field, tyi, txi),
        (shape((YL, 128, NX), BF16), shape((3, 3, C, 3 * C), F32), shape((C, 1), F32)),
        (2,),
        [pltpu.VMEM((512, 128), F32), pltpu.VMEM((1024, 128), F32)],
        flops=1 << 28,
        nbytes=4 << 20,
    )
    return (
        grad_field.reshape(features.shape),
        grad_spectral.reshape(spectral_weight.shape),
        grad_kernel,
        grad_bias.reshape(C),
    )


def solution(mesh):
    return jax.shard_map(
        on_device,
        mesh=mesh,
        in_specs=(
            P("gy", "gz", None, None),
            P("gy", "gz", None, None),
            P("gz", None, "gy"),
            P(),
            P(),
        ),
        out_specs=(P("gy", "gz", None, None), P("gz", None, "gy"), P(), P()),
        check_vma=False,
    )
```

```python
import functools
import math

import jax
import jax.numpy as jnp
import ml_dtypes
import numpy as np
from jax import lax
from jax.experimental import pallas as pl
from jax.experimental.pallas import tpu as pltpu
from jax.sharding import PartitionSpec as P

NX, NY, NZ = 512, 64, 64
C = 32
GY, GZ = 8, 16
YL, ZL = 8, 4
KXL = 4
LINE_ROWS = 64
MODE_ROWS = 16
GRAD_ROWS = 32
TAIL_ROWS = 8
SCALE = 1.0 / math.sqrt(NX * NY * NZ)
F32, BF16 = jnp.float32, jnp.bfloat16
LARGE = 60 * 1024 * 1024
SMALL = 16 * 1024 * 1024


def freqs(count, length):
    index = np.arange(count)
    return np.where(index < count // 2, index, length - count + index)


def angle(a, b, length):
    return 2.0 * math.pi / length * ((a[:, None] * b[None, :]) % length)


def split_np(table):
    high = table.astype(ml_dtypes.bfloat16)
    low = (table - high.astype(np.float64)).astype(ml_dtypes.bfloat16)
    return high, low


def x_forward_table():
    turn = angle(np.arange(32), np.arange(NX), NX)
    both = np.stack([np.cos(turn), -np.sin(turn)], 0).reshape(2, GY, KXL, NX)
    return both.transpose(1, 0, 2, 3).reshape(64, NX).astype(ml_dtypes.bfloat16)


def x_inverse_table():
    turn = angle(np.arange(32), np.arange(NX), NX)
    both = np.stack([np.cos(turn), -np.sin(turn)], 1).reshape(64, NX)
    high, low = split_np(both)
    return np.concatenate([high, low, high], 0)


def rotation(turn, sign):
    cos, sin = np.cos(turn), sign * np.sin(turn)
    return np.stack([np.stack([cos, -sin], -1), np.stack([sin, cos], -1)], 1)


def y_forward_table():
    turn = angle(freqs(32, NY), np.arange(NY), NY)
    table = rotation(turn, -1.0).reshape(GZ, 2, 2, NY, 2)
    full = np.einsum("gkpyq,ab->gakpyqb", table, np.eye(KXL)).reshape(256, 512)
    return np.stack(split_np(full))


def z_forward_table():
    turn = angle(freqs(32, NZ), np.arange(NZ), NZ)
    table = SCALE * rotation(turn, -1.0).reshape(32, 2, GZ, ZL, 2)
    full = np.einsum("kpgzq,ab->pakzbqg", table, np.eye(2)).reshape(128, 256)
    return np.stack(split_np(full))


def z_inverse_table():
    turn = angle(np.arange(NZ), freqs(32, NZ), NZ)
    table = SCALE * rotation(turn, 1.0).reshape(GZ, ZL, 2, 32, 2)
    full = np.einsum("gzpkq,ab->gapzqbk", table, np.eye(2)).reshape(256, 128)
    return np.stack(split_np(full))


def y_inverse_table():
    turn = angle(np.arange(NY), freqs(32, NY), NY)
    table = rotation(turn, 1.0).reshape(GY, YL, 2, GZ, 2, 2)
    full = np.einsum("dypgkq,ab->dapygkqb", table, np.eye(ZL)).reshape(512, 256)
    return np.stack(split_np(full))


def split(value):
    high = value.astype(BF16)
    return high, (value - high.astype(F32)).astype(BF16)


def dot(a, b):
    return jnp.dot(a, b, preferred_element_type=F32)


def dot_nt(a, b):
    return lax.dot_general(a, b, (((1,), (1,)), ((), ())), preferred_element_type=F32)


def dot_tn(a, b):
    return lax.dot_general(a, b, (((0,), (0,)), ((), ())), preferred_element_type=F32)


def lane_of(shape):
    return lax.broadcasted_iota(jnp.int32, shape, len(shape) - 1)


def swap_blocks(parts):
    lane = lane_of(parts[0].shape)
    half = lane < 64
    p0, p1, p2, p3 = parts
    q0 = jnp.where(half, p0, pltpu.roll(p2, 64, 1))
    q2 = jnp.where(half, pltpu.roll(p0, 64, 1), p2)
    q1 = jnp.where(half, p1, pltpu.roll(p3, 64, 1))
    q3 = jnp.where(half, pltpu.roll(p1, 64, 1), p3)
    even = (lane & 32) == 0
    out = []
    for lo, hi in ((q0, q1), (q2, q3)):
        out.append(jnp.where(even, lo, pltpu.roll(hi, 32, 1)))
        out.append(jnp.where(even, pltpu.roll(lo, 96, 1), hi))
    return out


def pack_lines(lines, send_ref):
    for g in range(GY):
        block = jnp.concatenate([line[g * 8 : g * 8 + 8] for line in lines], 0)
        send_ref[g, 0:LINE_ROWS] = block.astype(BF16)


def collect_spectrum(recv_ref, table_ref, rows_ref):
    rows_ref[...] = recv_ref[:, 0:MODE_ROWS].astype(F32).reshape(256, 128)
    turned = []
    for j in range(4):
        turned.append(
            swap_blocks([rows_ref[pl.ds(k * 4 + j, GZ, stride=16), :] for k in range(KXL)])
        )
    joined = jnp.concatenate([turned[j][z] for z in range(ZL) for j in range(4)], 0).astype(BF16)
    return dot(table_ref[0], joined) + dot(table_ref[1], joined)


def z_inverse(modes, table_ref):
    high, low = split(modes)
    return dot(table_ref[0], high) + dot(table_ref[1], high) + dot(table_ref[0], low)


def gain_lanes():
    lane = lane_of((128, 128))
    first = jnp.logical_and(lane < 32, lax.axis_index("gy") == 0)
    return jnp.where(first, 1.0, 2.0).astype(F32)


def repeat_matrix():
    row = lax.broadcasted_iota(jnp.int32, (64, 1024), 0) & 31
    return jnp.where(row == lane_of((64, 1024)) // 32, 1.0, 0.0).astype(BF16)


def spread(spectrum, k, matrix):
    high, low = split(spectrum[:, k * 32 : k * 32 + 32])
    return dot(jnp.concatenate([high, low], 1), matrix)


def fold_tiles(value):
    total = value[:, 0:128]
    for t in range(1, 8):
        total = total + value[:, t * 128 : t * 128 + 128]
    total = total + pltpu.roll(total, 64, 1)
    return total + pltpu.roll(total, 32, 1)


def place_fields(recv_ref, field_ref):
    for g in range(GY):
        block = recv_ref[g, 0:LINE_ROWS].astype(F32)
        turned = swap_blocks([block[z * 16 : z * 16 + 16] for z in range(ZL)])
        for k in range(KXL):
            for part in range(2):
                field_ref[pl.ds((g * 4 + k) * 2 + part, YL, stride=64), :] = turned[k][
                    part * 8 : part * 8 + 8
                ]


def x_inverse(field, table):
    high, low = split(field)
    return dot_tn(jnp.concatenate([high, high, low], 0), table)


def shift_right(value):
    return jnp.where(lane_of(value.shape) == 0, 0.0, pltpu.roll(value, 1, 1))


def shift_left(value):
    return jnp.where(lane_of(value.shape) == NX - 1, 0.0, pltpu.roll(value, NX - 1, 1))


def begin(copies, sems):
    started = [pltpu.make_async_copy(src, dst, sems.at[n]) for n, (src, dst) in enumerate(copies)]
    for copy in started:
        copy.start()
    return started


def finish(copies):
    for copy in copies:
        copy.wait()


def face_copies(field, front_ref, back_ref, first_ref, last_ref):
    return [
        (field.at[:, 0:32], front_ref),
        (field.at[:, 96:128], back_ref),
        (field.at[0], first_ref),
        (field.at[YL - 1], last_ref),
    ]


def analyse_kernel(own_ref, tx_hbm, send_ref, front_ref, back_ref, first_ref, last_ref, field, tx, in_sems, out_sems):
    fetched = begin([(tx_hbm, tx)] + [(own_ref.at[y], field.at[y]) for y in range(YL)], in_sems)
    fetched[0].wait()
    lines = []
    for y in range(YL):
        fetched[1 + y].wait()
        lines.append(dot_nt(tx[...], field[y]))
    faces = begin(face_copies(field, front_ref, back_ref, first_ref, last_ref), out_sems)
    pack_lines(lines, send_ref)
    finish(faces)


def y_kernel(recv_ref, table_ref, send_ref):
    lines = recv_ref[:, 0:LINE_ROWS].reshape(512, 128)
    out = dot(table_ref[0], lines) + dot(table_ref[1], lines)
    send_ref[:, 0:MODE_ROWS] = out.astype(BF16).reshape(GZ, MODE_ROWS, 128)


def y_back_kernel(recv_ref, table_ref, send_ref, sums_ref, tail_ref):
    y_kernel(recv_ref, table_ref, send_ref)
    total = jnp.zeros((2 * GRAD_ROWS, 128), F32)
    for g in range(GY):
        total = total + recv_ref[g, LINE_ROWS : LINE_ROWS + 2 * GRAD_ROWS].astype(F32)
    sums_ref[...] = total[0:GRAD_ROWS] + total[GRAD_ROWS : 2 * GRAD_ROWS]
    tail_ref[...] = jnp.zeros_like(tail_ref)
    for r in range(2):
        rows = sums_ref[pl.ds(r, GZ, stride=2), :]
        high = rows.astype(BF16).astype(F32)
        tail_ref[pl.ds(r, GZ, stride=TAIL_ROWS), :] = high
        tail_ref[pl.ds(r + 2, GZ, stride=TAIL_ROWS), :] = rows - high
    tail = tail_ref[...].reshape(GZ, TAIL_ROWS, 128)
    send_ref[:, MODE_ROWS : MODE_ROWS + TAIL_ROWS] = tail.astype(BF16)


def spread_kernel(recv_ref, table_ref, send_ref):
    modes = recv_ref[:, 0:MODE_ROWS].reshape(256, 128)
    out = dot(table_ref[0], modes) + dot(table_ref[1], modes)
    send_ref[:, 0:LINE_ROWS] = out.astype(BF16).reshape(GY, LINE_ROWS, 128)


def spread_back_kernel(recv_ref, table_ref, send_ref, tail_ref, both_ref):
    spread_kernel(recv_ref, table_ref, send_ref)
    tail = recv_ref[:, MODE_ROWS : MODE_ROWS + TAIL_ROWS].astype(F32)
    tail_ref[...] = tail.reshape(GZ * TAIL_ROWS, 128)
    for r in range(2):
        both_ref[pl.ds(r, GZ, stride=2), :] = tail_ref[pl.ds(r, GZ, stride=TAIL_ROWS), :]
        both_ref[pl.ds(GRAD_ROWS + r, GZ, stride=2), :] = tail_ref[pl.ds(r + 2, GZ, stride=TAIL_ROWS), :]
    both = both_ref[...].astype(BF16)
    for g in range(GY):
        send_ref[g, LINE_ROWS : LINE_ROWS + 2 * GRAD_ROWS] = both


def edges_kernel(own_first_ref, own_last_ref, zlo_ref, zhi_ref, first_ref, last_ref):
    for y, own, row in ((0, own_first_ref, first_ref), (YL - 1, own_last_ref, last_ref)):
        row[0:32] = zlo_ref[y]
        row[32:160] = own[...]
        row[160:192] = zhi_ref[y]


def pad_copies(pad, own_ref, zlo_ref, zhi_ref, ylo_ref, yhi_ref):
    return [
        (own_ref, pad.at[1:9, 32:160]),
        (zlo_ref, pad.at[1:9, 0:32]),
        (zhi_ref, pad.at[1:9, 160:192]),
        (ylo_ref, pad.at[0]),
        (yhi_ref, pad.at[9]),
    ]


def mix_kernel(recv_ref, weight_ref, tzf_ref, tzi_ref, send_ref, spec_ref, rows_ref):
    spectrum = collect_spectrum(recv_ref, tzf_ref, rows_ref)
    spec_ref[...] = spectrum
    matrix = repeat_matrix()
    lane = lane_of((64, 128)) // 32
    real = jnp.zeros((64, 128), F32)
    imag = jnp.zeros((64, 128), F32)
    for k in range(KXL):
        wide = spread(spectrum, k, matrix)
        w_re = weight_ref[:, k * 2048 : k * 2048 + 1024].astype(F32)
        w_im = weight_ref[:, k * 2048 + 1024 : k * 2048 + 2048].astype(F32)
        s_re, s_im = wide[0:64], wide[64:128]
        real = jnp.where(lane == k, fold_tiles(s_re * w_re - s_im * w_im), real)
        imag = jnp.where(lane == k, fold_tiles(s_re * w_im + s_im * w_re), imag)
    modes = jnp.concatenate([real, imag], 0) * gain_lanes()
    send_ref[...] = z_inverse(modes, tzi_ref).astype(BF16).reshape(GZ, MODE_ROWS, 128)


def build_taps(kernel_ref, taps, flip):
    zero = jnp.zeros((C, C), F32)
    row = lax.broadcasted_iota(jnp.int32, (C, C), 0)
    eye = jnp.where(row == lane_of((C, C)), 1.0, 0.0).astype(BF16)
    tap = {}
    for dy in range(3):
        for dz in range(3):
            if flip:
                turned = dot_tn(kernel_ref[2 - dy, 2 - dz], eye)
                for dx in range(3):
                    tap[dx, dy, dz] = turned[(2 - dx) * C : (2 - dx) * C + C]
            else:
                whole = kernel_ref[dy, dz].astype(F32)
                for dx in range(3):
                    tap[dx, dy, dz] = whole[:, dx * C : dx * C + C]
    for dx in range(3):
        for z in range(ZL):
            parts = [
                tap[dx, dy, zin - z] if 0 <= zin - z < 3 else zero
                for dy in range(3)
                for zin in range(ZL + 2)
            ]
            row = (dx * ZL + z) * C
            taps[row : row + C, :] = jnp.concatenate(parts, 1).astype(BF16)


def conv_kernel(
    flip, own_ref, zlo_ref, zhi_ref, ylo_ref, yhi_ref, kernel_hbm, bias_hbm, out_ref,
    pad, taps, buffer, kernel_ref, bias_ref, in_sems, out_sems,
):
    fetched = begin(
        [(kernel_hbm, kernel_ref), (bias_hbm, bias_ref)]
        + pad_copies(pad, own_ref, zlo_ref, zhi_ref, ylo_ref, yhi_ref),
        in_sems,
    )
    finish(fetched[0:2])
    build_taps(kernel_ref, taps, flip)
    if not flip:
        row = lax.broadcasted_iota(jnp.int32, (128, C), 0) & 31
        picked = jnp.where(row == lane_of((128, C)), bias_ref[...], 0.0)
        bias = jnp.sum(picked, axis=1, keepdims=True)
    finish(fetched[2:])

    def step(y, carry):
        window = pad[pl.ds(y, 3)].reshape(576, NX)
        wide = dot(taps[...], window)
        total = wide[128:256] + shift_right(wide[0:128]) + shift_left(wide[256:384])
        buffer[y] = total if flip else total + bias
        pltpu.make_async_copy(buffer.at[y], out_ref.at[y], out_sems.at[y]).start()
        return carry

    lax.fori_loop(0, YL, step, 0)
    for y in range(YL):
        pltpu.make_async_copy(buffer.at[y], out_ref.at[y], out_sems.at[y]).wait()


def slope_kernel(
    recv_ref, local_ref, cot_ref, txi_hbm, slope_ref, front_ref, back_ref, first_ref, last_ref,
    recv, local, cot, txi, field_ref, slopes, in_sems, out_sems,
):
    fetched = begin(
        [(recv_ref, recv), (txi_hbm, txi)]
        + [(local_ref.at[y], local.at[y]) for y in range(YL)]
        + [(cot_ref.at[y], cot.at[y]) for y in range(YL)],
        in_sems,
    )
    fetched[0].wait()
    place_fields(recv, field_ref)
    fetched[1].wait()
    root = math.sqrt(2.0 / math.pi)
    copies = []
    for y in range(YL):
        fetched[2 + y].wait()
        fetched[2 + YL + y].wait()
        pre = x_inverse(field_ref[y * 64 : y * 64 + 64], txi[...]) + local[y]
        square = pre * pre
        bent = jnp.tanh(root * pre * (1.0 + 0.044715 * square))
        rate = 0.5 * (1.0 + bent) + 0.5 * root * pre * (1.0 - bent * bent) * (
            1.0 + 3.0 * 0.044715 * square
        )
        slopes[y] = (cot[y].astype(F32) * rate).astype(BF16)
        copies += begin([(slopes.at[y], slope_ref.at[y])], out_sems.at[y : y + 1])
    copies += begin(face_copies(slopes, front_ref, back_ref, first_ref, last_ref), out_sems.at[YL : YL + 4])
    finish(copies)


def back_kernel(
    slope_ref, own_ref, zlo_ref, zhi_ref, ylo_ref, yhi_ref, tx_hbm, send_ref,
    slopes, pad, tx, sums_ref, in_sems,
):
    fetched = begin(
        [(tx_hbm, tx)]
        + [(slope_ref.at[y], slopes.at[y]) for y in range(YL)]
        + pad_copies(pad, own_ref, zlo_ref, zhi_ref, ylo_ref, yhi_ref),
        in_sems,
    )
    sums_ref[...] = jnp.zeros_like(sums_ref)
    finish(fetched)
    lines = []
    bias = jnp.zeros((128, 1), F32)
    for y in range(YL):
        slope = slopes[y]
        lines.append(dot_nt(tx[...], slope))
        wide = slope.astype(F32)
        bias = bias + jnp.sum(wide, axis=1, keepdims=True)
        three = jnp.concatenate(
            [shift_left(wide).astype(BF16), slope, shift_right(wide).astype(BF16)], 0
        )
        sums_ref[...] += dot_nt(three, pad[y : y + 3].reshape(576, NX))
    pack_lines(lines, send_ref)
    bias32 = bias[0:32] + bias[32:64] + bias[64:96] + bias[96:128]
    pieces = []
    for dx in range(3):
        for dy in range(3):
            total = jnp.zeros((C, 96), F32)
            for z in range(ZL):
                row = (dx * ZL + z) * C
                col = dy * 192 + z * C
                total = total + sums_ref[row : row + C, col : col + 96]
            pieces += [total[:, dz * C : dz * C + C] for dz in range(3)]
    pieces.append(jnp.broadcast_to(bias32, (C, C)))
    for g in range(GY):
        if g < 7:
            rows = jnp.concatenate(pieces[4 * g : 4 * g + 4], 1)
        else:
            rows = jnp.zeros((C, 128), F32)
        high, low = split(rows)
        send_ref[g, LINE_ROWS : LINE_ROWS + GRAD_ROWS] = high
        send_ref[g, LINE_ROWS + GRAD_ROWS : LINE_ROWS + 2 * GRAD_ROWS] = low


def adjoint_kernel(recv_ref, weight_ref, tzf_ref, tzi_ref, send_ref, spec_ref, rows_ref):
    spectrum = collect_spectrum(recv_ref, tzf_ref, rows_ref)
    spec_ref[...] = spectrum
    row = lax.broadcasted_iota(jnp.int32, (1024, 128), 0) // 32
    lane = lane_of((1024, 128))
    gather = []
    for k in range(KXL):
        w_re = weight_ref[:, k * 2048 : k * 2048 + 1024].astype(F32)
        w_im = weight_ref[:, k * 2048 + 1024 : k * 2048 + 2048].astype(F32)
        own = spectrum[:, k * 32 : k * 32 + 32]
        four = jnp.concatenate([own] * 4, 1)
        wide = jnp.concatenate([four] * 8, 1)
        b_re, b_im = wide[0:64], wide[64:128]
        both = jnp.concatenate([b_re * w_re + b_im * w_im, b_im * w_re - b_re * w_im], 0)
        matrix = jnp.where(row + k * 32 == lane, 1.0, 0.0).astype(BF16)
        high, low = split(both)
        gather.append(dot(high, matrix) + dot(low, matrix))
    modes = (gather[0] + gather[1] + gather[2] + gather[3]) * gain_lanes()
    block = z_inverse(modes, tzi_ref).astype(BF16)
    send_ref[:, 0:MODE_ROWS] = block.reshape(GZ, MODE_ROWS, 128)
    total = jnp.sum(recv_ref[:, MODE_ROWS : MODE_ROWS + TAIL_ROWS].astype(F32), axis=0)
    total = total + pltpu.roll(total, TAIL_ROWS - 2, 0)
    high = total.astype(BF16).astype(F32)
    part = lax.broadcasted_iota(jnp.int32, (TAIL_ROWS, 128), 0)
    low = jnp.where(part < 4, pltpu.roll(total - high, 2, 0), 0.0)
    tail = jnp.where(part < 2, high, low).astype(BF16)
    send_ref[:, MODE_ROWS : MODE_ROWS + TAIL_ROWS] = jnp.broadcast_to(tail[None], (GZ, TAIL_ROWS, 128))


def outer_kernel(spec_ref, back_ref, out_hbm, out_ref, sems):
    copies = []
    matrix = repeat_matrix()
    gain = gain_lanes()
    spectrum = spec_ref[...]
    back = back_ref[...] * gain
    for k in range(KXL):
        wide = spread(spectrum, k, matrix)
        s_re, s_im = wide[0:64], wide[64:128]
        own = back[:, k * 32 : k * 32 + 32]
        four = jnp.concatenate([own] * 4, 1)
        tiled = jnp.concatenate([four] * 8, 1)
        b_re, b_im = tiled[0:64], tiled[64:128]
        out_ref[:, k * 2048 : k * 2048 + 1024] = s_re * b_re + s_im * b_im
        out_ref[:, k * 2048 + 1024 : k * 2048 + 2048] = s_re * b_im - s_im * b_re
        part = slice(k * 2048, k * 2048 + 2048)
        copies += begin([(out_ref.at[:, part], out_hbm.at[:, part])], sems.at[k : k + 1])
    finish(copies)


def final_kernel(
    recv_ref, conv_ref, txi_hbm, grad_ref, kernel_ref, bias_ref,
    recv, conv, txi, field_ref, grads, in_sems, out_sems,
):
    fetched = begin(
        [(recv_ref, recv), (txi_hbm, txi)] + [(conv_ref.at[y], conv.at[y]) for y in range(YL)], in_sems
    )
    fetched[0].wait()
    place_fields(recv, field_ref)
    fetched[1].wait()
    copies = []
    for y in range(YL):
        back = x_inverse(field_ref[y * 64 : y * 64 + 64], txi[...])
        fetched[2 + y].wait()
        grads[y] = (back + conv[y]).astype(BF16)
        copies += begin([(grads.at[y], grad_ref.at[y])], out_sems.at[y : y + 1])
    piece = []
    for g in range(7):
        high = recv[g, LINE_ROWS : LINE_ROWS + GRAD_ROWS].astype(F32)
        low = recv[g, LINE_ROWS + GRAD_ROWS : LINE_ROWS + 2 * GRAD_ROWS].astype(F32)
        rows = SCALE * (high + low)
        piece += [rows[:, j * C : j * C + C] for j in range(4)]
    for dy in range(3):
        for dz in range(3):
            kernel_ref[dy, dz] = jnp.concatenate([piece[dx * 9 + dy * 3 + dz] for dx in range(3)], 1)
    row = lax.broadcasted_iota(jnp.int32, (C, C), 0)
    bias_ref[...] = jnp.sum(jnp.where(row == lane_of((C, C)), piece[27], 0.0), axis=0, keepdims=True)
    finish(copies)


AUTO, HBM = pl.BlockSpec(), pl.BlockSpec(memory_space=pltpu.HBM)


def vmem(dims, kind):
    return pltpu.VMEM(dims, kind)


def sems(count):
    return pltpu.SemaphoreType.DMA((count,))


def shape(dims, kind):
    return jax.ShapeDtypeStruct(dims, kind)


def call(body, ins, outs, scratch, room, *operands):
    return pl.pallas_call(
        body,
        in_specs=ins,
        out_specs=[spec for spec, _ in outs],
        out_shape=[kind for _, kind in outs],
        scratch_shapes=scratch,
        compiler_params=pltpu.CompilerParams(vmem_limit_bytes=room),
    )(*operands)


def exchange(blocks, axis):
    return lax.all_to_all(blocks, axis, 0, 0, tiled=True)


FIELD = shape((YL, 128, NX), BF16)
SIDE = shape((YL, 32, NX), BF16)
FACE = shape((128, NX), BF16)
EDGE = shape((192, NX), BF16)
PAD = vmem((YL + 2, 192, NX), BF16)


def after(value, *others):
    return lax.optimization_barrier((value, *others))[0]


def z_halos(front, back):
    zlo = lax.ppermute(back, "gz", [(i, i + 1) for i in range(GZ - 1)])
    zhi = lax.ppermute(front, "gz", [(i + 1, i) for i in range(GZ - 1)])
    return zlo, zhi


def y_edges(first, last, zlo, zhi):
    return call(edges_kernel, [AUTO] * 4, [(AUTO, EDGE)] * 2, [], SMALL, first, last, zlo, zhi)


def y_halos(first, last):
    ylo = lax.ppermute(last, "gy", [(i, i + 1) for i in range(GY - 1)])
    yhi = lax.ppermute(first, "gy", [(i + 1, i) for i in range(GY - 1)])
    return ylo, yhi


def conv(flip, own, halo, kernel, bias):
    return call(
        functools.partial(conv_kernel, flip),
        [HBM] * 7,
        [(HBM, shape((YL, 128, NX), F32))],
        [
            PAD, vmem((384, 576), BF16), vmem((YL, 128, NX), F32),
            vmem((3, 3, C, 3 * C), BF16), vmem((1, C), F32), sems(7), sems(YL),
        ],
        LARGE,
        own, *halo, kernel, bias,
    )[0]


def on_device(features, cotangent, spectral_weight, kernel_weight, channel_bias):
    own = features.reshape(YL, 128, NX)
    cot = cotangent.reshape(YL, 128, NX)
    weight = spectral_weight.reshape(64, 8192)
    bias = channel_bias.reshape(1, C)
    tx = jnp.asarray(x_forward_table())
    txi = jnp.asarray(x_inverse_table())
    ty = jnp.asarray(y_forward_table())
    tyi = jnp.asarray(y_inverse_table())
    tzf = jnp.asarray(z_forward_table())
    tzi = jnp.asarray(z_inverse_table())
    faces_out = [(HBM, SIDE)] * 2 + [(HBM, FACE)] * 2
    spectrum_out = (AUTO, shape((128, 128), F32))

    def lines_out(rows):
        return AUTO, shape((GY, rows, 128), BF16)

    def modes_out(rows):
        return AUTO, shape((GZ, rows, 128), BF16)

    both_rows = LINE_ROWS + 2 * GRAD_ROWS
    tail_rows = MODE_ROWS + TAIL_ROWS
    send, front, back, first, last = call(
        analyse_kernel,
        [HBM] * 2,
        [lines_out(LINE_ROWS)] + faces_out,
        [vmem((YL, 128, NX), BF16), vmem((64, NX), BF16), sems(1 + YL), sems(4)],
        LARGE,
        own, tx,
    )
    recv = exchange(send, "gy")

    zlo, zhi = z_halos(front, back)
    (send,) = call(y_kernel, [AUTO] * 2, [modes_out(MODE_ROWS)], [], SMALL, recv, ty)
    recv = exchange(send, "gz")
    send, spectrum = call(
        mix_kernel,
        [AUTO] * 4,
        [modes_out(MODE_ROWS), spectrum_out],
        [vmem((256, 128), F32)],
        SMALL,
        recv, weight, tzf, tzi,
    )
    halo = (zlo, zhi, *y_halos(*y_edges(after(first, send), last, zlo, zhi)))
    recv = exchange(send, "gz")
    recv, *halo = lax.optimization_barrier((recv, *halo))
    (send,) = call(spread_kernel, [AUTO] * 2, [lines_out(LINE_ROWS)], [], SMALL, recv, tyi)
    local = conv(False, after(own, send), halo, kernel_weight, bias)
    recv = exchange(send, "gy")
    slope, front, back, first, last = call(
        slope_kernel,
        [HBM] * 4,
        [(HBM, FIELD)] + faces_out,
        [
            vmem((GY, LINE_ROWS, 128), BF16), vmem((YL, 128, NX), F32), vmem((YL, 128, NX), BF16),
            vmem((192, NX), BF16), vmem((512, 128), F32), vmem((YL, 128, NX), BF16),
            sems(2 + 2 * YL), sems(YL + 4),
        ],
        LARGE,
        recv, local, cot, txi,
    )
    (send,) = call(
        back_kernel,
        [HBM] * 7,
        [lines_out(both_rows)],
        [
            vmem((YL, 128, NX), BF16), PAD, vmem((64, NX), BF16), vmem((384, 576), F32), sems(6 + YL),
        ],
        LARGE,
        slope, own, *halo, tx,
    )
    recv = exchange(send, "gy")

    zlo, zhi = z_halos(front, back)
    (send,) = call(
        y_back_kernel,
        [AUTO] * 2,
        [modes_out(tail_rows)],
        [vmem((GRAD_ROWS, 128), F32), vmem((GZ * TAIL_ROWS, 128), F32)],
        SMALL,
        recv, ty,
    )
    recv = exchange(send, "gz")
    send, back = call(
        adjoint_kernel,
        [AUTO] * 4,
        [modes_out(tail_rows), spectrum_out],
        [vmem((256, 128), F32)],
        SMALL,
        recv, weight, tzf, tzi,
    )
    halo = (zlo, zhi, *y_halos(*y_edges(after(first, send), last, zlo, zhi)))
    recv = exchange(send, "gz")
    (grad_spectral,) = call(
        outer_kernel,
        [AUTO] * 2,
        [(HBM, shape((64, 8192), F32))],
        [vmem((64, 8192), F32), sems(KXL)],
        LARGE,
        after(spectrum, send), back,
    )
    recv, grad_spectral, *halo = lax.optimization_barrier((recv, grad_spectral, *halo))
    (send,) = call(
        spread_back_kernel,
        [AUTO] * 2,
        [lines_out(both_rows)],
        [vmem((GZ * TAIL_ROWS, 128), F32), vmem((2 * GRAD_ROWS, 128), F32)],
        SMALL,
        recv, tyi,
    )
    recv = exchange(send, "gy")
    conv_field = conv(True, after(slope, send), halo, kernel_weight, bias)
    grad_field, grad_kernel, grad_bias = call(
        final_kernel,
        [HBM] * 3,
        [(HBM, FIELD), (AUTO, shape((3, 3, C, 3 * C), F32)), (AUTO, shape((1, C), F32))],
        [
            vmem((GY, both_rows, 128), BF16), vmem((YL, 128, NX), F32), vmem((192, NX), BF16),
            vmem((512, 128), F32), vmem((YL, 128, NX), BF16), sems(2 + YL), sems(YL),
        ],
        LARGE,
        recv, conv_field, txi,
    )
    return (
        grad_field.reshape(features.shape),
        grad_spectral.reshape(spectral_weight.shape),
        grad_kernel,
        grad_bias.reshape(C),
    )


def solution(mesh):
    return jax.shard_map(
        on_device,
        mesh=mesh,
        in_specs=(
            P("gy", "gz", None, None),
            P("gy", "gz", None, None),
            P("gz", None, "gy"),
            P(),
            P(),
        ),
        out_specs=(P("gy", "gz", None, None), P("gz", None, "gy"), P(), P()),
        check_vma=False,
    )
```

```python
import functools
import math

import jax
import jax.numpy as jnp
import ml_dtypes
import numpy as np
from jax import lax
from jax.experimental import pallas as pl
from jax.experimental.pallas import tpu as pltpu
from jax.sharding import PartitionSpec as P

NX, NY, NZ = 512, 64, 64
C = 32
GY, GZ = 8, 16
YL, ZL = 8, 4
KXL = 4
LINE_ROWS = 64
MODE_ROWS = 16
GRAD_ROWS = 32
TAIL_ROWS = 8
SCALE = 1.0 / math.sqrt(NX * NY * NZ)
F32, BF16 = jnp.float32, jnp.bfloat16
LARGE = 60 * 1024 * 1024
SMALL = 16 * 1024 * 1024


def freqs(count, length):
    index = np.arange(count)
    return np.where(index < count // 2, index, length - count + index)


def angle(a, b, length):
    return 2.0 * math.pi / length * ((a[:, None] * b[None, :]) % length)


def split_np(table):
    high = table.astype(ml_dtypes.bfloat16)
    low = (table - high.astype(np.float64)).astype(ml_dtypes.bfloat16)
    return high, low


def x_forward_table():
    turn = angle(np.arange(32), np.arange(NX), NX)
    both = np.stack([np.cos(turn), -np.sin(turn)], 0).reshape(2, GY, KXL, NX)
    return both.transpose(1, 0, 2, 3).reshape(64, NX).astype(ml_dtypes.bfloat16)


def x_inverse_table():
    turn = angle(np.arange(32), np.arange(NX), NX)
    both = np.stack([np.cos(turn), -np.sin(turn)], 1).reshape(64, NX)
    high, low = split_np(both)
    return np.concatenate([high, low, high], 0)


def rotation(turn, sign):
    cos, sin = np.cos(turn), sign * np.sin(turn)
    return np.stack([np.stack([cos, -sin], -1), np.stack([sin, cos], -1)], 1)


def y_forward_table():
    turn = angle(freqs(32, NY), np.arange(NY), NY)
    table = rotation(turn, -1.0).reshape(GZ, 2, 2, NY, 2)
    full = np.einsum("gkpyq,ab->gakpyqb", table, np.eye(KXL)).reshape(256, 512)
    return np.stack(split_np(full))


def z_forward_table():
    turn = angle(freqs(32, NZ), np.arange(NZ), NZ)
    table = SCALE * rotation(turn, -1.0).reshape(32, 2, GZ, ZL, 2)
    full = np.einsum("kpgzq,ab->pakzbqg", table, np.eye(2)).reshape(128, 256)
    return np.stack(split_np(full))


def z_inverse_table():
    turn = angle(np.arange(NZ), freqs(32, NZ), NZ)
    table = SCALE * rotation(turn, 1.0).reshape(GZ, ZL, 2, 32, 2)
    full = np.einsum("gzpkq,ab->gapzqbk", table, np.eye(2)).reshape(256, 128)
    return np.stack(split_np(full))


def y_inverse_table():
    turn = angle(np.arange(NY), freqs(32, NY), NY)
    table = rotation(turn, 1.0).reshape(GY, YL, 2, GZ, 2, 2)
    full = np.einsum("dypgkq,ab->dapygkqb", table, np.eye(ZL)).reshape(512, 256)
    return np.stack(split_np(full))


def split(value):
    high = value.astype(BF16)
    return high, (value - high.astype(F32)).astype(BF16)


def dot(a, b):
    return jnp.dot(a, b, preferred_element_type=F32)


def dot_nt(a, b):
    return lax.dot_general(a, b, (((1,), (1,)), ((), ())), preferred_element_type=F32)


def dot_tn(a, b):
    return lax.dot_general(a, b, (((0,), (0,)), ((), ())), preferred_element_type=F32)


def lane_of(shape):
    return lax.broadcasted_iota(jnp.int32, shape, len(shape) - 1)


def swap_blocks(parts):
    lane = lane_of(parts[0].shape)
    half = lane < 64
    p0, p1, p2, p3 = parts
    q0 = jnp.where(half, p0, pltpu.roll(p2, 64, 1))
    q2 = jnp.where(half, pltpu.roll(p0, 64, 1), p2)
    q1 = jnp.where(half, p1, pltpu.roll(p3, 64, 1))
    q3 = jnp.where(half, pltpu.roll(p1, 64, 1), p3)
    even = (lane & 32) == 0
    out = []
    for lo, hi in ((q0, q1), (q2, q3)):
        out.append(jnp.where(even, lo, pltpu.roll(hi, 32, 1)))
        out.append(jnp.where(even, pltpu.roll(lo, 96, 1), hi))
    return out


def pack_lines(lines, send_ref):
    for g in range(GY):
        block = jnp.concatenate([line[g * 8 : g * 8 + 8] for line in lines], 0)
        send_ref[g, 0:LINE_ROWS] = block.astype(BF16)


def collect_spectrum(recv_ref, table_ref, rows_ref):
    rows_ref[...] = recv_ref[:, 0:MODE_ROWS].astype(F32).reshape(256, 128)
    turned = []
    for j in range(4):
        turned.append(
            swap_blocks([rows_ref[pl.ds(k * 4 + j, GZ, stride=16), :] for k in range(KXL)])
        )
    joined = jnp.concatenate([turned[j][z] for z in range(ZL) for j in range(4)], 0).astype(BF16)
    return dot(table_ref[0], joined) + dot(table_ref[1], joined)


def z_inverse(modes, table_ref):
    high, low = split(modes)
    return dot(table_ref[0], high) + dot(table_ref[1], high) + dot(table_ref[0], low)


def gain_lanes():
    lane = lane_of((128, 128))
    first = jnp.logical_and(lane < 32, lax.axis_index("gy") == 0)
    return jnp.where(first, 1.0, 2.0).astype(F32)


def repeat_matrix():
    row = lax.broadcasted_iota(jnp.int32, (64, 1024), 0) & 31
    return jnp.where(row == lane_of((64, 1024)) // 32, 1.0, 0.0).astype(BF16)


def spread(spectrum, k, matrix):
    high, low = split(spectrum[:, k * 32 : k * 32 + 32])
    return dot(jnp.concatenate([high, low], 1), matrix)


def fold_tiles(value):
    total = value[:, 0:128]
    for t in range(1, 8):
        total = total + value[:, t * 128 : t * 128 + 128]
    total = total + pltpu.roll(total, 64, 1)
    return total + pltpu.roll(total, 32, 1)


def place_fields(recv_ref, field_ref):
    for g in range(GY):
        block = recv_ref[g, 0:LINE_ROWS].astype(F32)
        turned = swap_blocks([block[z * 16 : z * 16 + 16] for z in range(ZL)])
        for k in range(KXL):
            for part in range(2):
                field_ref[pl.ds((g * 4 + k) * 2 + part, YL, stride=64), :] = turned[k][
                    part * 8 : part * 8 + 8
                ]


def x_inverse(field, table):
    high, low = split(field)
    return dot_tn(jnp.concatenate([high, high, low], 0), table)


def shift_right(value):
    return jnp.where(lane_of(value.shape) == 0, 0.0, pltpu.roll(value, 1, 1))


def shift_left(value):
    return jnp.where(lane_of(value.shape) == NX - 1, 0.0, pltpu.roll(value, NX - 1, 1))


def begin(copies, sems):
    started = [pltpu.make_async_copy(src, dst, sems.at[n]) for n, (src, dst) in enumerate(copies)]
    for copy in started:
        copy.start()
    return started


def finish(copies):
    for copy in copies:
        copy.wait()


def face_copies(field, front_ref, back_ref, first_ref, last_ref):
    return [
        (field.at[:, 0:32], front_ref),
        (field.at[:, 96:128], back_ref),
        (field.at[0], first_ref),
        (field.at[YL - 1], last_ref),
    ]


def analyse_kernel(own_ref, tx_hbm, send_ref, front_ref, back_ref, first_ref, last_ref, field, tx, in_sems, out_sems):
    finish(begin([(tx_hbm, tx), (own_ref, field)], in_sems))
    faces = begin(face_copies(field, front_ref, back_ref, first_ref, last_ref), out_sems)
    lines = [dot_nt(tx[...], field[y]) for y in range(YL)]
    pack_lines(lines, send_ref)
    send_ref[:, LINE_ROWS:] = jnp.zeros((GY, LINE_ROWS, 128), BF16)
    finish(faces)


def y_kernel(recv_ref, table_ref, send_ref):
    lines = recv_ref[:, 0:LINE_ROWS].reshape(512, 128)
    out = dot(table_ref[0], lines) + dot(table_ref[1], lines)
    send_ref[:, 0:MODE_ROWS] = out.astype(BF16).reshape(GZ, MODE_ROWS, 128)


def y_back_kernel(recv_ref, table_ref, send_ref, sums_ref, tail_ref):
    y_kernel(recv_ref, table_ref, send_ref)
    total = jnp.zeros((2 * GRAD_ROWS, 128), F32)
    for g in range(GY):
        total = total + recv_ref[g, LINE_ROWS : LINE_ROWS + 2 * GRAD_ROWS].astype(F32)
    sums_ref[...] = total[0:GRAD_ROWS] + total[GRAD_ROWS : 2 * GRAD_ROWS]
    tail_ref[...] = jnp.zeros_like(tail_ref)
    for r in range(2):
        rows = sums_ref[pl.ds(r, GZ, stride=2), :]
        high = rows.astype(BF16).astype(F32)
        tail_ref[pl.ds(r, GZ, stride=TAIL_ROWS), :] = high
        tail_ref[pl.ds(r + 2, GZ, stride=TAIL_ROWS), :] = rows - high
    tail = tail_ref[...].reshape(GZ, TAIL_ROWS, 128)
    send_ref[:, MODE_ROWS : MODE_ROWS + TAIL_ROWS] = tail.astype(BF16)


def spread_kernel(recv_ref, table_ref, send_ref):
    modes = recv_ref[:, 0:MODE_ROWS].reshape(256, 128)
    out = dot(table_ref[0], modes) + dot(table_ref[1], modes)
    send_ref[:, 0:LINE_ROWS] = out.astype(BF16).reshape(GY, LINE_ROWS, 128)


def spread_back_kernel(recv_ref, table_ref, send_ref, tail_ref, both_ref):
    spread_kernel(recv_ref, table_ref, send_ref)
    tail = recv_ref[:, MODE_ROWS : MODE_ROWS + TAIL_ROWS].astype(F32)
    tail_ref[...] = tail.reshape(GZ * TAIL_ROWS, 128)
    for r in range(2):
        both_ref[pl.ds(r, GZ, stride=2), :] = tail_ref[pl.ds(r, GZ, stride=TAIL_ROWS), :]
        both_ref[pl.ds(GRAD_ROWS + r, GZ, stride=2), :] = tail_ref[pl.ds(r + 2, GZ, stride=TAIL_ROWS), :]
    both = both_ref[...].astype(BF16)
    for g in range(GY):
        send_ref[g, LINE_ROWS : LINE_ROWS + 2 * GRAD_ROWS] = both


def edges_kernel(own_first_ref, own_last_ref, zlo_ref, zhi_ref, first_ref, last_ref):
    for y, own, row in ((0, own_first_ref, first_ref), (YL - 1, own_last_ref, last_ref)):
        row[0:32] = zlo_ref[y]
        row[32:160] = own[...]
        row[160:192] = zhi_ref[y]


def pad_copies(pad, own_ref, zlo_ref, zhi_ref, ylo_ref, yhi_ref):
    return [
        (own_ref, pad.at[1:9, 32:160]),
        (zlo_ref, pad.at[1:9, 0:32]),
        (zhi_ref, pad.at[1:9, 160:192]),
        (ylo_ref, pad.at[0]),
        (yhi_ref, pad.at[YL + 1]),
    ]


def mix_kernel(recv_ref, weight_ref, tzf_ref, tzi_ref, send_ref, spec_ref, rows_ref):
    spectrum = collect_spectrum(recv_ref, tzf_ref, rows_ref)
    spec_ref[...] = spectrum
    matrix = repeat_matrix()
    lane = lane_of((64, 128)) // 32
    real = jnp.zeros((64, 128), F32)
    imag = jnp.zeros((64, 128), F32)
    for k in range(KXL):
        wide = spread(spectrum, k, matrix)
        w_re = weight_ref[:, k * 2048 : k * 2048 + 1024].astype(F32)
        w_im = weight_ref[:, k * 2048 + 1024 : k * 2048 + 2048].astype(F32)
        s_re, s_im = wide[0:64], wide[64:128]
        real = jnp.where(lane == k, fold_tiles(s_re * w_re - s_im * w_im), real)
        imag = jnp.where(lane == k, fold_tiles(s_re * w_im + s_im * w_re), imag)
    modes = jnp.concatenate([real, imag], 0) * gain_lanes()
    send_ref[:, MODE_ROWS:] = jnp.zeros((GZ, 3 * MODE_ROWS, 128), BF16)
    send_ref[:, 0:MODE_ROWS] = z_inverse(modes, tzi_ref).astype(BF16).reshape(GZ, MODE_ROWS, 128)


def build_taps(kernel_ref, taps, flip):
    row = lax.broadcasted_iota(jnp.int32, (C, C), 0)
    eye = jnp.where(row == lane_of((C, C)), 1.0, 0.0).astype(BF16)
    tap = {}
    for dy in range(3):
        for dz in range(3):
            if flip:
                turned = dot_tn(kernel_ref[2 - dy, 2 - dz], eye)
                for dx in range(3):
                    tap[dx, dy, dz] = turned[(2 - dx) * C : (2 - dx) * C + C]
            else:
                whole = kernel_ref[dy, dz].astype(F32)
                for dx in range(3):
                    tap[dx, dy, dz] = whole[:, dx * C : dx * C + C]
    for dx in range(3):
        parts = []
        for dy in range(3):
            parts += [tap[dx, dy, dz] for dz in range(3)] + [jnp.zeros((C, 96), F32)]
        base = jnp.concatenate(parts + [jnp.zeros((C, 64), F32)], 1)
        for z in range(ZL):
            row = (dx * ZL + z) * C
            moved = pltpu.roll(base, z * C, 1) if z else base
            taps[row : row + C, :] = moved[:, 0:576].astype(BF16)


def conv_kernel(
    flip, own_ref, zlo_ref, zhi_ref, ylo_ref, yhi_ref, kernel_hbm, bias_hbm, out_ref,
    pad, taps, buffer, kernel_ref, bias_ref, in_sems, out_sems,
):
    fetched = begin(
        [(kernel_hbm, kernel_ref), (bias_hbm, bias_ref)]
        + pad_copies(pad, own_ref, zlo_ref, zhi_ref, ylo_ref, yhi_ref),
        in_sems,
    )
    finish(fetched[0:2])
    padded = fetched[2:]
    build_taps(kernel_ref, taps, flip)
    if not flip:
        row = lax.broadcasted_iota(jnp.int32, (128, C), 0) & 31
        picked = jnp.where(row == lane_of((128, C)), bias_ref[...], 0.0)
        bias = jnp.sum(picked, axis=1, keepdims=True)
    finish(padded)
    copies = []
    for y in range(YL):
        wide = dot(taps[...], pad[y : y + 3].reshape(576, NX))
        total = wide[128:256] + shift_right(wide[0:128]) + shift_left(wide[256:384])
        buffer[y] = (total if flip else total + bias).astype(BF16)
        if y % 4 == 3:
            half = slice(y - 3, y + 1)
            copies += begin([(buffer.at[half], out_ref.at[half])], out_sems.at[y // 4 : y // 4 + 1])
    finish(copies)


def slope_kernel(
    recv_ref, local_ref, cot_ref, own_ref, zlo_ref, zhi_ref, ylo_ref, yhi_ref, txi_hbm, tx_hbm,
    slope_ref, front_ref, back_ref, first_ref, last_ref, send_ref,
    recv, local, cot, pad, txi, tx, field_ref, slopes, sums_ref, in_sems, out_sems,
):
    fetched = begin(
        [(recv_ref, recv), (txi_hbm, txi), (tx_hbm, tx), (local_ref, local), (cot_ref, cot)]
        + pad_copies(pad, own_ref, zlo_ref, zhi_ref, ylo_ref, yhi_ref),
        in_sems,
    )
    fetched[0].wait()
    place_fields(recv, field_ref)
    finish(fetched[1:5])
    root = math.sqrt(2.0 / math.pi)
    lines = []
    for y in range(YL):
        pre = x_inverse(field_ref[y * 64 : y * 64 + 64], txi[...]) + local[y].astype(F32)
        square = pre * pre
        bent = jnp.tanh(root * pre * (1.0 + 0.044715 * square))
        rate = 0.5 * (1.0 + bent) + 0.5 * root * pre * (1.0 - bent * bent) * (
            1.0 + 3.0 * 0.044715 * square
        )
        slope = (cot[y].astype(F32) * rate).astype(BF16)
        slopes[y] = slope
        lines.append(dot_nt(tx[...], slope))
    copies = begin(
        face_copies(slopes, front_ref, back_ref, first_ref, last_ref) + [(slopes, slope_ref)], out_sems
    )
    pack_lines(lines, send_ref)
    finish(fetched[5:])
    bias = jnp.zeros((128, 1), F32)
    for start in range(0, YL, 4):
        left, right = [], []
        for y in range(start, start + 4):
            slope = slopes[y]
            wide = slope.astype(F32)
            bias = bias + jnp.sum(wide, axis=1, keepdims=True)
            left.append(
                jnp.concatenate([shift_left(wide).astype(BF16), slope, shift_right(wide).astype(BF16)], 0)
            )
            right.append(pad[y : y + 3].reshape(576, NX))
        part = dot_nt(jnp.concatenate(left, 1), jnp.concatenate(right, 1))
        sums_ref[...] = part if start == 0 else sums_ref[...] + part
    bias32 = bias[0:32] + bias[32:64] + bias[64:96] + bias[96:128]
    pieces = []
    for dx in range(3):
        for dy in range(3):
            total = jnp.zeros((C, 96), F32)
            for z in range(ZL):
                row = (dx * ZL + z) * C
                col = dy * 192 + z * C
                total = total + sums_ref[row : row + C, col : col + 96]
            pieces += [total[:, dz * C : dz * C + C] for dz in range(3)]
    pieces.append(jnp.broadcast_to(bias32, (C, C)))
    for g in range(GY):
        if g < 7:
            rows = jnp.concatenate(pieces[4 * g : 4 * g + 4], 1)
        else:
            rows = jnp.zeros((C, 128), F32)
        high, low = split(rows)
        send_ref[g, LINE_ROWS : LINE_ROWS + GRAD_ROWS] = high
        send_ref[g, LINE_ROWS + GRAD_ROWS : LINE_ROWS + 2 * GRAD_ROWS] = low
    finish(copies)


def adjoint_kernel(recv_ref, weight_ref, tzf_ref, tzi_ref, send_ref, spec_ref, rows_ref):
    spectrum = collect_spectrum(recv_ref, tzf_ref, rows_ref)
    spec_ref[...] = spectrum
    row = lax.broadcasted_iota(jnp.int32, (1024, 128), 0) // 32
    lane = lane_of((1024, 128))
    gather = []
    for k in range(KXL):
        w_re = weight_ref[:, k * 2048 : k * 2048 + 1024].astype(F32)
        w_im = weight_ref[:, k * 2048 + 1024 : k * 2048 + 2048].astype(F32)
        own = spectrum[:, k * 32 : k * 32 + 32]
        four = jnp.concatenate([own] * 4, 1)
        wide = jnp.concatenate([four] * 8, 1)
        b_re, b_im = wide[0:64], wide[64:128]
        both = jnp.concatenate([b_re * w_re + b_im * w_im, b_im * w_re - b_re * w_im], 0)
        matrix = jnp.where(row + k * 32 == lane, 1.0, 0.0).astype(BF16)
        high, low = split(both)
        gather.append(dot(high, matrix) + dot(low, matrix))
    modes = (gather[0] + gather[1] + gather[2] + gather[3]) * gain_lanes()
    send_ref[:, MODE_ROWS:] = jnp.zeros((GZ, 3 * MODE_ROWS, 128), BF16)
    block = z_inverse(modes, tzi_ref).astype(BF16)
    send_ref[:, 0:MODE_ROWS] = block.reshape(GZ, MODE_ROWS, 128)
    total = jnp.sum(recv_ref[:, MODE_ROWS : MODE_ROWS + TAIL_ROWS].astype(F32), axis=0)
    total = total + pltpu.roll(total, TAIL_ROWS - 2, 0)
    high = total.astype(BF16).astype(F32)
    part = lax.broadcasted_iota(jnp.int32, (TAIL_ROWS, 128), 0)
    low = jnp.where(part < 4, pltpu.roll(total - high, 2, 0), 0.0)
    tail = jnp.where(part < 2, high, low).astype(BF16)
    send_ref[:, MODE_ROWS : MODE_ROWS + TAIL_ROWS] = jnp.broadcast_to(tail[None], (GZ, TAIL_ROWS, 128))


def outer_kernel(spec_ref, back_ref, out_hbm, out_ref, sems):
    copies = []
    matrix = repeat_matrix()
    gain = gain_lanes()
    spectrum = spec_ref[...]
    back = back_ref[...] * gain
    for k in range(KXL):
        wide = spread(spectrum, k, matrix)
        s_re, s_im = wide[0:64], wide[64:128]
        own = back[:, k * 32 : k * 32 + 32]
        four = jnp.concatenate([own] * 4, 1)
        tiled = jnp.concatenate([four] * 8, 1)
        b_re, b_im = tiled[0:64], tiled[64:128]
        out_ref[:, k * 2048 : k * 2048 + 1024] = s_re * b_re + s_im * b_im
        out_ref[:, k * 2048 + 1024 : k * 2048 + 2048] = s_re * b_im - s_im * b_re
        part = slice(k * 2048, k * 2048 + 2048)
        copies += begin([(out_ref.at[:, part], out_hbm.at[:, part])], sems.at[k : k + 1])
    finish(copies)


def final_kernel(
    recv_ref, conv_ref, txi_hbm, grad_ref, kernel_ref, bias_ref,
    recv, conv, txi, field_ref, grads, in_sems, out_sems,
):
    fetched = begin([(recv_ref, recv), (txi_hbm, txi), (conv_ref, conv)], in_sems)
    fetched[0].wait()
    place_fields(recv, field_ref)
    finish(fetched[1:])
    copies = []
    for y in range(YL):
        back = x_inverse(field_ref[y * 64 : y * 64 + 64], txi[...])
        grads[y] = (back + conv[y].astype(F32)).astype(BF16)
        if y % 4 == 3:
            half = slice(y - 3, y + 1)
            copies += begin([(grads.at[half], grad_ref.at[half])], out_sems.at[y // 4 : y // 4 + 1])
    piece = []
    for g in range(7):
        high = recv[g, LINE_ROWS : LINE_ROWS + GRAD_ROWS].astype(F32)
        low = recv[g, LINE_ROWS + GRAD_ROWS : LINE_ROWS + 2 * GRAD_ROWS].astype(F32)
        rows = SCALE * (high + low)
        piece += [rows[:, j * C : j * C + C] for j in range(4)]
    for dy in range(3):
        for dz in range(3):
            kernel_ref[dy, dz] = jnp.concatenate([piece[dx * 9 + dy * 3 + dz] for dx in range(3)], 1)
    row = lax.broadcasted_iota(jnp.int32, (C, C), 0)
    bias_ref[...] = jnp.sum(jnp.where(row == lane_of((C, C)), piece[27], 0.0), axis=0, keepdims=True)
    finish(copies)


AUTO, HBM = pl.BlockSpec(), pl.BlockSpec(memory_space=pltpu.HBM)


def vmem(dims, kind):
    return pltpu.VMEM(dims, kind)


def sems(count):
    return pltpu.SemaphoreType.DMA((count,))


def shape(dims, kind):
    return jax.ShapeDtypeStruct(dims, kind)


def call(body, ins, outs, scratch, room, *operands):
    return pl.pallas_call(
        body,
        in_specs=ins,
        out_specs=[spec for spec, _ in outs],
        out_shape=[kind for _, kind in outs],
        scratch_shapes=scratch,
        compiler_params=pltpu.CompilerParams(vmem_limit_bytes=room),
    )(*operands)


def exchange(blocks, axis):
    return lax.all_to_all(blocks, axis, 0, 0, tiled=True)


FIELD = shape((YL, 128, NX), BF16)
SIDE = shape((YL, 32, NX), BF16)
FACE = shape((128, NX), BF16)
EDGE = shape((192, NX), BF16)
PAD = vmem((YL + 2, 192, NX), BF16)


def after(value, *others):
    return lax.optimization_barrier((value, *others))[0]


def z_halos(front, back):
    zlo = lax.ppermute(back, "gz", [(i, i + 1) for i in range(GZ - 1)])
    zhi = lax.ppermute(front, "gz", [(i + 1, i) for i in range(GZ - 1)])
    return zlo, zhi


def y_edges(first, last, zlo, zhi):
    return call(edges_kernel, [AUTO] * 4, [(AUTO, EDGE)] * 2, [], SMALL, first, last, zlo, zhi)


def y_halos(first, last):
    ylo = lax.ppermute(last, "gy", [(i, i + 1) for i in range(GY - 1)])
    yhi = lax.ppermute(first, "gy", [(i + 1, i) for i in range(GY - 1)])
    return ylo, yhi


def conv(flip, own, halo, kernel, bias):
    return call(
        functools.partial(conv_kernel, flip),
        [HBM] * 7,
        [(HBM, FIELD)],
        [
            PAD, vmem((384, 576), BF16), vmem((YL, 128, NX), BF16),
            vmem((3, 3, C, 3 * C), BF16), vmem((1, C), F32), sems(7), sems(2),
        ],
        LARGE,
        own, *halo, kernel, bias,
    )[0]


def on_device(features, cotangent, spectral_weight, kernel_weight, channel_bias):
    own = features.reshape(YL, 128, NX)
    cot = cotangent.reshape(YL, 128, NX)
    weight = spectral_weight.reshape(64, 8192)
    bias = channel_bias.reshape(1, C)
    tx = jnp.asarray(x_forward_table())
    txi = jnp.asarray(x_inverse_table())
    ty = jnp.asarray(y_forward_table())
    tyi = jnp.asarray(y_inverse_table())
    tzf = jnp.asarray(z_forward_table())
    tzi = jnp.asarray(z_inverse_table())
    faces_out = [(HBM, SIDE)] * 2 + [(HBM, FACE)] * 2
    spectrum_out = (AUTO, shape((128, 128), F32))

    def lines_out(rows):
        return AUTO, shape((GY, rows, 128), BF16)

    def modes_out(rows):
        return AUTO, shape((GZ, rows, 128), BF16)

    both_rows = LINE_ROWS + 2 * GRAD_ROWS
    tail_rows = MODE_ROWS + TAIL_ROWS
    send, front, back, first, last = call(
        analyse_kernel,
        [HBM] * 2,
        [lines_out(2 * LINE_ROWS)] + faces_out,
        [vmem((YL, 128, NX), BF16), vmem((64, NX), BF16), sems(2), sems(4)],
        LARGE,
        own, tx,
    )
    recv = exchange(send, "gy")

    zlo, zhi = z_halos(front, back)
    (send,) = call(y_kernel, [AUTO] * 2, [modes_out(MODE_ROWS)], [], SMALL, recv, ty)
    recv = exchange(send, "gz")
    send, spectrum = call(
        mix_kernel,
        [AUTO] * 4,
        [modes_out(4 * MODE_ROWS), spectrum_out],
        [vmem((256, 128), F32)],
        SMALL,
        recv, weight, tzf, tzi,
    )
    halo = (zlo, zhi, *y_halos(*y_edges(after(first, send), last, zlo, zhi)))
    recv = exchange(send, "gz")
    recv, *halo = lax.optimization_barrier((recv, *halo))
    (send,) = call(spread_kernel, [AUTO] * 2, [lines_out(LINE_ROWS)], [], SMALL, recv, tyi)
    local = conv(False, after(own, send), halo, kernel_weight, bias)
    recv = exchange(send, "gy")
    slope, front, back, first, last, send = call(
        slope_kernel,
        [HBM] * 10,
        [(HBM, FIELD)] + faces_out + [lines_out(both_rows)],
        [
            vmem((GY, LINE_ROWS, 128), BF16), vmem((YL, 128, NX), BF16), vmem((YL, 128, NX), BF16), PAD,
            vmem((192, NX), BF16), vmem((64, NX), BF16), vmem((512, 128), F32), vmem((YL, 128, NX), BF16),
            vmem((384, 576), F32), sems(10), sems(5),
        ],
        LARGE,
        recv, local, cot, own, *halo, txi, tx,
    )
    recv = exchange(send, "gy")

    zlo, zhi = z_halos(front, back)
    (send,) = call(
        y_back_kernel,
        [AUTO] * 2,
        [modes_out(tail_rows)],
        [vmem((GRAD_ROWS, 128), F32), vmem((GZ * TAIL_ROWS, 128), F32)],
        SMALL,
        recv, ty,
    )
    recv = exchange(send, "gz")
    send, back = call(
        adjoint_kernel,
        [AUTO] * 4,
        [modes_out(4 * MODE_ROWS), spectrum_out],
        [vmem((256, 128), F32)],
        SMALL,
        recv, weight, tzf, tzi,
    )
    halo = (zlo, zhi, *y_halos(*y_edges(after(first, send), last, zlo, zhi)))
    recv = exchange(send, "gz")
    (grad_spectral,) = call(
        outer_kernel,
        [AUTO] * 2,
        [(HBM, shape((64, 8192), F32))],
        [vmem((64, 8192), F32), sems(KXL)],
        LARGE,
        after(spectrum, send), back,
    )
    recv, grad_spectral, *halo = lax.optimization_barrier((recv, grad_spectral, *halo))
    (send,) = call(
        spread_back_kernel,
        [AUTO] * 2,
        [lines_out(both_rows)],
        [vmem((GZ * TAIL_ROWS, 128), F32), vmem((2 * GRAD_ROWS, 128), F32)],
        SMALL,
        recv, tyi,
    )
    recv = exchange(send, "gy")
    conv_field = conv(True, after(slope, send), halo, kernel_weight, bias)
    grad_field, grad_kernel, grad_bias = call(
        final_kernel,
        [HBM] * 3,
        [(HBM, FIELD), (AUTO, shape((3, 3, C, 3 * C), F32)), (AUTO, shape((1, C), F32))],
        [
            vmem((GY, both_rows, 128), BF16), vmem((YL, 128, NX), BF16), vmem((192, NX), BF16),
            vmem((512, 128), F32), vmem((YL, 128, NX), BF16), sems(3), sems(2),
        ],
        LARGE,
        recv, conv_field, txi,
    )
    return (
        grad_field.reshape(features.shape),
        grad_spectral.reshape(spectral_weight.shape),
        grad_kernel,
        grad_bias.reshape(C),
    )


def solution(mesh):
    return jax.shard_map(
        on_device,
        mesh=mesh,
        in_specs=(
            P("gy", "gz", None, None),
            P("gy", "gz", None, None),
            P("gz", None, "gy"),
            P(),
            P(),
        ),
        out_specs=(P("gy", "gz", None, None), P("gz", None, "gy"), P(), P()),
        check_vma=False,
    )
```

```python
import functools
import math

import jax
import jax.numpy as jnp
import ml_dtypes
import numpy as np
from jax import lax
from jax.experimental import pallas as pl
from jax.experimental.pallas import tpu as pltpu
from jax.sharding import PartitionSpec as P

NX, NY, NZ = 512, 64, 64
C = 32
GY, GZ = 8, 16
YL, ZL = 8, 4
KXL = 4
LINE_ROWS = 64
MODE_ROWS = 16
GRAD_ROWS = 32
TAIL_ROWS = 8
SCALE = 1.0 / math.sqrt(NX * NY * NZ)
F32, BF16 = jnp.float32, jnp.bfloat16
LARGE = 60 * 1024 * 1024
MEDIUM = 48 * 1024 * 1024
SMALL = 16 * 1024 * 1024


def freqs(count, length):
    index = np.arange(count)
    return np.where(index < count // 2, index, length - count + index)


def angle(a, b, length):
    return 2.0 * math.pi / length * ((a[:, None] * b[None, :]) % length)


def split_np(table):
    high = table.astype(ml_dtypes.bfloat16)
    low = (table - high.astype(np.float64)).astype(ml_dtypes.bfloat16)
    return high, low


def x_forward_table():
    turn = angle(np.arange(32), np.arange(NX), NX)
    both = np.stack([np.cos(turn), -np.sin(turn)], 0).reshape(2, GY, KXL, NX)
    return both.transpose(1, 0, 2, 3).reshape(64, NX).astype(ml_dtypes.bfloat16)


def x_inverse_table():
    turn = angle(np.arange(32), np.arange(NX), NX)
    both = np.stack([np.cos(turn), -np.sin(turn)], 1).reshape(64, NX)
    high, low = split_np(both)
    return np.concatenate([high, low, high], 0)


def rotation(turn, sign):
    cos, sin = np.cos(turn), sign * np.sin(turn)
    return np.stack([np.stack([cos, -sin], -1), np.stack([sin, cos], -1)], 1)


def y_forward_table():
    turn = angle(freqs(32, NY), np.arange(NY), NY)
    table = rotation(turn, -1.0).reshape(GZ, 2, 2, NY, 2)
    full = np.einsum("gkpyq,ab->gakpyqb", table, np.eye(KXL)).reshape(256, 512)
    return full


def z_forward_table():
    turn = angle(freqs(32, NZ), np.arange(NZ), NZ)
    table = SCALE * rotation(turn, -1.0).reshape(32, 2, GZ, ZL, 2)
    full = np.einsum("kpgzq,ab->pakzbqg", table, np.eye(2)).reshape(128, 256)
    return full


def z_inverse_table():
    turn = angle(np.arange(NZ), freqs(32, NZ), NZ)
    table = SCALE * rotation(turn, 1.0).reshape(GZ, ZL, 2, 32, 2)
    full = np.einsum("gzpkq,ab->gapzqbk", table, np.eye(2)).reshape(256, 128)
    return full


def y_inverse_table():
    turn = angle(np.arange(NY), freqs(32, NY), NY)
    table = rotation(turn, 1.0).reshape(GY, YL, 2, GZ, 2, 2)
    full = np.einsum("dypgkq,ab->dapygkqb", table, np.eye(ZL)).reshape(512, 256)
    return full


def side_by_side(table):
    return np.concatenate(split_np(table), 1)


def joint_table():
    z_inverse = side_by_side(z_inverse_table())
    return np.concatenate(
        [
            *split_np(y_forward_table()),
            side_by_side(y_inverse_table()),
            side_by_side(z_forward_table()),
            np.concatenate([z_inverse, np.zeros_like(z_inverse)], 1),
        ],
        0,
    )


Y_INVERSE, Z_FORWARD, Z_INVERSE = 512, 1024, 1152


def split(value):
    high = value.astype(BF16)
    return high, (value - high.astype(F32)).astype(BF16)


def dot(a, b):
    return jnp.dot(a, b, preferred_element_type=F32)


def dot_nt(a, b):
    return lax.dot_general(a, b, (((1,), (1,)), ((), ())), preferred_element_type=F32)


def dot_tn(a, b):
    return lax.dot_general(a, b, (((0,), (0,)), ((), ())), preferred_element_type=F32)


def lane_of(shape):
    return lax.broadcasted_iota(jnp.int32, shape, len(shape) - 1)


def swap_blocks(parts):
    lane = lane_of(parts[0].shape)
    half = lane < 64
    p0, p1, p2, p3 = parts
    q0 = jnp.where(half, p0, pltpu.roll(p2, 64, 1))
    q2 = jnp.where(half, pltpu.roll(p0, 64, 1), p2)
    q1 = jnp.where(half, p1, pltpu.roll(p3, 64, 1))
    q3 = jnp.where(half, pltpu.roll(p1, 64, 1), p3)
    even = (lane & 32) == 0
    out = []
    for lo, hi in ((q0, q1), (q2, q3)):
        out.append(jnp.where(even, lo, pltpu.roll(hi, 32, 1)))
        out.append(jnp.where(even, pltpu.roll(lo, 96, 1), hi))
    return out


def pack_lines(lines, send_ref):
    for g in range(GY):
        block = jnp.concatenate([line[g * 8 : g * 8 + 8] for line in lines], 0)
        send_ref[g, 0:LINE_ROWS] = block.astype(BF16)


def collect_spectrum(recv_ref, table_ref, rows_ref):
    rows_ref[...] = recv_ref[:, 0:MODE_ROWS].astype(F32).reshape(256, 128)
    turned = []
    for j in range(4):
        turned.append(
            swap_blocks([rows_ref[pl.ds(k * 4 + j, GZ, stride=16), :] for k in range(KXL)])
        )
    joined = jnp.concatenate([turned[j][z] for z in range(ZL) for j in range(4)], 0).astype(BF16)
    rows = slice(Z_FORWARD, Z_FORWARD + 128)
    return dot(table_ref[rows, 0:256], joined) + dot(table_ref[rows, 256:512], joined)


def z_inverse(modes, table_ref):
    high, low = split(modes)
    rows = slice(Z_INVERSE, Z_INVERSE + 256)
    table_high, table_low = table_ref[rows, 0:128], table_ref[rows, 128:256]
    return dot(table_high, high) + dot(table_low, high) + dot(table_high, low)


def gain_lanes():
    lane = lane_of((128, 128))
    first = jnp.logical_and(lane < 32, lax.axis_index("gy") == 0)
    return jnp.where(first, 1.0, 2.0).astype(F32)


def repeat_matrix():
    row = lax.broadcasted_iota(jnp.int32, (64, 1024), 0) & 31
    return jnp.where(row == lane_of((64, 1024)) // 32, 1.0, 0.0).astype(BF16)


def spread(spectrum, k, matrix):
    high, low = split(spectrum[:, k * 32 : k * 32 + 32])
    return dot(jnp.concatenate([high, low], 1), matrix)


def fold_tiles(value):
    total = value[:, 0:128]
    for t in range(1, 8):
        total = total + value[:, t * 128 : t * 128 + 128]
    total = total + pltpu.roll(total, 64, 1)
    return total + pltpu.roll(total, 32, 1)


def place_fields(recv_ref, field_ref):
    for g in range(GY):
        block = recv_ref[g, 0:LINE_ROWS].astype(F32)
        turned = swap_blocks([block[z * 16 : z * 16 + 16] for z in range(ZL)])
        for k in range(KXL):
            for part in range(2):
                field_ref[pl.ds((g * 4 + k) * 2 + part, YL, stride=64), :] = turned[k][
                    part * 8 : part * 8 + 8
                ]


def x_inverse(field, table):
    high, low = split(field)
    return dot_tn(jnp.concatenate([high, high, low], 0), table)


def shift_right(value):
    return jnp.where(lane_of(value.shape) == 0, 0.0, pltpu.roll(value, 1, 1))


def shift_left(value):
    return jnp.where(lane_of(value.shape) == NX - 1, 0.0, pltpu.roll(value, NX - 1, 1))


def begin(copies, sems):
    started = [pltpu.make_async_copy(src, dst, sems.at[n]) for n, (src, dst) in enumerate(copies)]
    for copy in started:
        copy.start()
    return started


def finish(copies):
    for copy in copies:
        copy.wait()


def face_copies(field, front_ref, back_ref, first_ref, last_ref):
    return [
        (field.at[:, 0:32], front_ref),
        (field.at[:, 96:128], back_ref),
        (field.at[0], first_ref),
        (field.at[YL - 1], last_ref),
    ]


def analyse_kernel(own_ref, tx_hbm, send_ref, front_ref, back_ref, first_ref, last_ref, field, tx, in_sems, out_sems):
    finish(begin([(tx_hbm, tx), (own_ref, field)], in_sems))
    faces = begin(face_copies(field, front_ref, back_ref, first_ref, last_ref), out_sems)
    lines = [dot_nt(tx[...], field[y]) for y in range(YL)]
    pack_lines(lines, send_ref)
    send_ref[:, LINE_ROWS:] = jnp.zeros((GY, LINE_ROWS, 128), BF16)
    finish(faces)


def y_kernel(recv_ref, table_ref, send_ref):
    lines = recv_ref[:, 0:LINE_ROWS].reshape(512, 128)
    out = dot(table_ref[0:256], lines) + dot(table_ref[256:512], lines)
    send_ref[:, 0:MODE_ROWS] = out.astype(BF16).reshape(GZ, MODE_ROWS, 128)


def y_back_kernel(recv_ref, table_ref, send_ref, sums_ref, tail_ref):
    y_kernel(recv_ref, table_ref, send_ref)
    total = jnp.zeros((2 * GRAD_ROWS, 128), F32)
    for g in range(GY):
        total = total + recv_ref[g, LINE_ROWS : LINE_ROWS + 2 * GRAD_ROWS].astype(F32)
    sums_ref[...] = total[0:GRAD_ROWS] + total[GRAD_ROWS : 2 * GRAD_ROWS]
    tail_ref[...] = jnp.zeros_like(tail_ref)
    for r in range(2):
        rows = sums_ref[pl.ds(r, GZ, stride=2), :]
        high = rows.astype(BF16).astype(F32)
        tail_ref[pl.ds(r, GZ, stride=TAIL_ROWS), :] = high
        tail_ref[pl.ds(r + 2, GZ, stride=TAIL_ROWS), :] = rows - high
    tail = tail_ref[...].reshape(GZ, TAIL_ROWS, 128)
    send_ref[:, MODE_ROWS : MODE_ROWS + TAIL_ROWS] = tail.astype(BF16)


def spread_kernel(recv_ref, table_ref, send_ref):
    modes = recv_ref[:, 0:MODE_ROWS].reshape(256, 128)
    rows = slice(Y_INVERSE, Y_INVERSE + 512)
    out = dot(table_ref[rows, 0:256], modes) + dot(table_ref[rows, 256:512], modes)
    send_ref[:, 0:LINE_ROWS] = out.astype(BF16).reshape(GY, LINE_ROWS, 128)


def spread_back_kernel(recv_ref, table_ref, send_ref, tail_ref, both_ref):
    spread_kernel(recv_ref, table_ref, send_ref)
    tail = recv_ref[:, MODE_ROWS : MODE_ROWS + TAIL_ROWS].astype(F32)
    tail_ref[...] = tail.reshape(GZ * TAIL_ROWS, 128)
    for r in range(2):
        both_ref[pl.ds(r, GZ, stride=2), :] = tail_ref[pl.ds(r, GZ, stride=TAIL_ROWS), :]
        both_ref[pl.ds(GRAD_ROWS + r, GZ, stride=2), :] = tail_ref[pl.ds(r + 2, GZ, stride=TAIL_ROWS), :]
    both = both_ref[...].astype(BF16)
    for g in range(GY):
        send_ref[g, LINE_ROWS : LINE_ROWS + 2 * GRAD_ROWS] = both


def own_core():
    return lax.rem(lax.axis_index("gy"), 2)


def edges_kernel(own_first_ref, own_last_ref, zlo_ref, zhi_ref, inner_ref, outer_ref):
    first, last = [
        jnp.concatenate([zlo_ref[y], own[...], zhi_ref[y]], 0)
        for y, own in ((0, own_first_ref), (YL - 1, own_last_ref))
    ]
    even = own_core() == 0
    inner_ref[...] = jnp.where(even, last, first)
    outer_ref[...] = jnp.where(even, first, last)


def pad_copies(pad, own_ref, zlo_ref, zhi_ref, inner_ref, outer_ref):
    return [
        (own_ref, pad.at[1:9, 32:160]),
        (zlo_ref, pad.at[1:9, 0:32]),
        (zhi_ref, pad.at[1:9, 160:192]),
        (inner_ref, pad.at[(1 - own_core()) * (YL + 1)]),
        (outer_ref, pad.at[own_core() * (YL + 1)]),
    ]


def mix_kernel(recv_ref, weight_ref, table_ref, send_ref, spec_ref, rows_ref):
    spectrum = collect_spectrum(recv_ref, table_ref, rows_ref)
    spec_ref[...] = spectrum
    matrix = repeat_matrix()
    lane = lane_of((64, 128)) // 32
    real = jnp.zeros((64, 128), F32)
    imag = jnp.zeros((64, 128), F32)
    for k in range(KXL):
        wide = spread(spectrum, k, matrix)
        w_re = weight_ref[:, k * 2048 : k * 2048 + 1024].astype(F32)
        w_im = weight_ref[:, k * 2048 + 1024 : k * 2048 + 2048].astype(F32)
        s_re, s_im = wide[0:64], wide[64:128]
        real = jnp.where(lane == k, fold_tiles(s_re * w_re - s_im * w_im), real)
        imag = jnp.where(lane == k, fold_tiles(s_re * w_im + s_im * w_re), imag)
    modes = jnp.concatenate([real, imag], 0) * gain_lanes()
    send_ref[:, MODE_ROWS:] = jnp.zeros((GZ, 3 * MODE_ROWS, 128), BF16)
    send_ref[:, 0:MODE_ROWS] = z_inverse(modes, table_ref).astype(BF16).reshape(GZ, MODE_ROWS, 128)


def build_taps(kernel_ref, taps, flip):
    row = lax.broadcasted_iota(jnp.int32, (C, C), 0)
    eye = jnp.where(row == lane_of((C, C)), 1.0, 0.0).astype(BF16)
    tap = {}
    for dy in range(3):
        for dz in range(3):
            if flip:
                turned = dot_tn(kernel_ref[2 - dy, 2 - dz], eye)
                for dx in range(3):
                    tap[dx, dy, dz] = turned[(2 - dx) * C : (2 - dx) * C + C]
            else:
                whole = kernel_ref[dy, dz].astype(F32)
                for dx in range(3):
                    tap[dx, dy, dz] = whole[:, dx * C : dx * C + C]
    for dx in range(3):
        parts = []
        for dy in range(3):
            parts += [tap[dx, dy, dz] for dz in range(3)] + [jnp.zeros((C, 96), F32)]
        base = jnp.concatenate(parts + [jnp.zeros((C, 64), F32)], 1)
        for z in range(ZL):
            row = (dx * ZL + z) * C
            moved = pltpu.roll(base, z * C, 1) if z else base
            taps[row : row + C, :] = moved[:, 0:576].astype(BF16)


def conv_kernel(
    flip, own_ref, zlo_ref, zhi_ref, inner_ref, outer_ref, kernel_hbm, bias_hbm, out_ref,
    pad, taps, buffer, kernel_ref, bias_ref, in_sems, out_sems,
):
    fetched = begin(
        [(kernel_hbm, kernel_ref), (bias_hbm, bias_ref)]
        + pad_copies(pad, own_ref, zlo_ref, zhi_ref, inner_ref, outer_ref),
        in_sems,
    )
    finish(fetched[0:2])
    padded = fetched[2:]
    build_taps(kernel_ref, taps, flip)
    if not flip:
        row = lax.broadcasted_iota(jnp.int32, (128, C), 0) & 31
        picked = jnp.where(row == lane_of((128, C)), bias_ref[...], 0.0)
        bias = jnp.sum(picked, axis=1, keepdims=True)
    finish(padded)
    copies = []
    for y in range(YL):
        wide = dot(taps[...], pad[y : y + 3].reshape(576, NX))
        total = wide[128:256] + shift_right(wide[0:128]) + shift_left(wide[256:384])
        buffer[y] = (total if flip else total + bias).astype(BF16)
        if y % 4 == 3:
            half = slice(y - 3, y + 1)
            copies += begin([(buffer.at[half], out_ref.at[half])], out_sems.at[y // 4 : y // 4 + 1])
    finish(copies)


def slope_kernel(
    recv_ref, local_ref, cot_ref, own_ref, zlo_ref, zhi_ref, inner_ref, outer_ref, txi_hbm, tx_hbm,
    slope_ref, front_ref, back_ref, first_ref, last_ref, send_ref,
    recv, local, cot, pad, txi, tx, field_ref, slopes, sums_ref, in_sems, out_sems,
):
    fetched = begin(
        [(recv_ref, recv), (txi_hbm, txi), (tx_hbm, tx), (local_ref, local), (cot_ref, cot)]
        + pad_copies(pad, own_ref, zlo_ref, zhi_ref, inner_ref, outer_ref),
        in_sems,
    )
    fetched[0].wait()
    place_fields(recv, field_ref)
    finish(fetched[1:5])
    root = math.sqrt(2.0 / math.pi)
    lines = []
    for y in range(YL):
        pre = x_inverse(field_ref[y * 64 : y * 64 + 64], txi[...]) + local[y].astype(F32)
        square = pre * pre
        bent = jnp.tanh(root * pre * (1.0 + 0.044715 * square))
        rate = 0.5 * (1.0 + bent) + 0.5 * root * pre * (1.0 - bent * bent) * (
            1.0 + 3.0 * 0.044715 * square
        )
        slope = (cot[y].astype(F32) * rate).astype(BF16)
        slopes[y] = slope
        lines.append(dot_nt(tx[...], slope))
    copies = begin(
        face_copies(slopes, front_ref, back_ref, first_ref, last_ref) + [(slopes, slope_ref)], out_sems
    )
    pack_lines(lines, send_ref)
    finish(fetched[5:])
    bias = jnp.zeros((128, 1), F32)
    for start in range(0, YL, 4):
        left, right = [], []
        for y in range(start, start + 4):
            slope = slopes[y]
            wide = slope.astype(F32)
            bias = bias + jnp.sum(wide, axis=1, keepdims=True)
            left.append(
                jnp.concatenate([shift_left(wide).astype(BF16), slope, shift_right(wide).astype(BF16)], 0)
            )
            right.append(pad[y : y + 3].reshape(576, NX))
        part = dot_nt(jnp.concatenate(left, 1), jnp.concatenate(right, 1))
        sums_ref[...] = part if start == 0 else sums_ref[...] + part
    bias32 = bias[0:32] + bias[32:64] + bias[64:96] + bias[96:128]
    pieces = []
    for dx in range(3):
        for dy in range(3):
            total = jnp.zeros((C, 96), F32)
            for z in range(ZL):
                row = (dx * ZL + z) * C
                col = dy * 192 + z * C
                total = total + sums_ref[row : row + C, col : col + 96]
            pieces += [total[:, dz * C : dz * C + C] for dz in range(3)]
    pieces.append(jnp.broadcast_to(bias32, (C, C)))
    for g in range(GY):
        if g < 7:
            rows = jnp.concatenate(pieces[4 * g : 4 * g + 4], 1)
        else:
            rows = jnp.zeros((C, 128), F32)
        high, low = split(rows)
        send_ref[g, LINE_ROWS : LINE_ROWS + GRAD_ROWS] = high
        send_ref[g, LINE_ROWS + GRAD_ROWS : LINE_ROWS + 2 * GRAD_ROWS] = low
    finish(copies)


def adjoint_kernel(recv_ref, weight_ref, table_ref, send_ref, spec_ref, rows_ref):
    spectrum = collect_spectrum(recv_ref, table_ref, rows_ref)
    spec_ref[...] = spectrum
    row = lax.broadcasted_iota(jnp.int32, (1024, 128), 0) // 32
    lane = lane_of((1024, 128))
    gather = []
    for k in range(KXL):
        w_re = weight_ref[:, k * 2048 : k * 2048 + 1024].astype(F32)
        w_im = weight_ref[:, k * 2048 + 1024 : k * 2048 + 2048].astype(F32)
        own = spectrum[:, k * 32 : k * 32 + 32]
        four = jnp.concatenate([own] * 4, 1)
        wide = jnp.concatenate([four] * 8, 1)
        b_re, b_im = wide[0:64], wide[64:128]
        both = jnp.concatenate([b_re * w_re + b_im * w_im, b_im * w_re - b_re * w_im], 0)
        matrix = jnp.where(row + k * 32 == lane, 1.0, 0.0).astype(BF16)
        high, low = split(both)
        gather.append(dot(high, matrix) + dot(low, matrix))
    modes = (gather[0] + gather[1] + gather[2] + gather[3]) * gain_lanes()
    send_ref[:, MODE_ROWS:] = jnp.zeros((GZ, 3 * MODE_ROWS, 128), BF16)
    block = z_inverse(modes, table_ref).astype(BF16)
    send_ref[:, 0:MODE_ROWS] = block.reshape(GZ, MODE_ROWS, 128)
    total = jnp.sum(recv_ref[:, MODE_ROWS : MODE_ROWS + TAIL_ROWS].astype(F32), axis=0)
    total = total + pltpu.roll(total, TAIL_ROWS - 2, 0)
    high = total.astype(BF16).astype(F32)
    part = lax.broadcasted_iota(jnp.int32, (TAIL_ROWS, 128), 0)
    low = jnp.where(part < 4, pltpu.roll(total - high, 2, 0), 0.0)
    tail = jnp.where(part < 2, high, low).astype(BF16)
    send_ref[:, MODE_ROWS : MODE_ROWS + TAIL_ROWS] = jnp.broadcast_to(tail[None], (GZ, TAIL_ROWS, 128))


def outer_kernel(spec_ref, back_ref, out_hbm, out_ref, sems):
    copies = []
    matrix = repeat_matrix()
    gain = gain_lanes()
    spectrum = spec_ref[...]
    back = back_ref[...] * gain
    for k in range(KXL):
        wide = spread(spectrum, k, matrix)
        s_re, s_im = wide[0:64], wide[64:128]
        own = back[:, k * 32 : k * 32 + 32]
        four = jnp.concatenate([own] * 4, 1)
        tiled = jnp.concatenate([four] * 8, 1)
        b_re, b_im = tiled[0:64], tiled[64:128]
        out_ref[:, k * 2048 : k * 2048 + 1024] = s_re * b_re + s_im * b_im
        out_ref[:, k * 2048 + 1024 : k * 2048 + 2048] = s_re * b_im - s_im * b_re
        part = slice(k * 2048, k * 2048 + 2048)
        copies += begin([(out_ref.at[:, part], out_hbm.at[:, part])], sems.at[k : k + 1])
    finish(copies)


def final_kernel(
    recv_ref, conv_ref, txi_hbm, grad_ref, kernel_ref, bias_ref,
    recv, conv, txi, field_ref, grads, in_sems, out_sems,
):
    fetched = begin([(recv_ref, recv), (txi_hbm, txi), (conv_ref, conv)], in_sems)
    fetched[0].wait()
    place_fields(recv, field_ref)
    finish(fetched[1:])
    copies = []
    for y in range(YL):
        back = x_inverse(field_ref[y * 64 : y * 64 + 64], txi[...])
        grads[y] = (back + conv[y].astype(F32)).astype(BF16)
        if y % 4 == 3:
            half = slice(y - 3, y + 1)
            copies += begin([(grads.at[half], grad_ref.at[half])], out_sems.at[y // 4 : y // 4 + 1])
    piece = []
    for g in range(7):
        high = recv[g, LINE_ROWS : LINE_ROWS + GRAD_ROWS].astype(F32)
        low = recv[g, LINE_ROWS + GRAD_ROWS : LINE_ROWS + 2 * GRAD_ROWS].astype(F32)
        rows = SCALE * (high + low)
        piece += [rows[:, j * C : j * C + C] for j in range(4)]
    for dy in range(3):
        for dz in range(3):
            kernel_ref[dy, dz] = jnp.concatenate([piece[dx * 9 + dy * 3 + dz] for dx in range(3)], 1)
    row = lax.broadcasted_iota(jnp.int32, (C, C), 0)
    bias_ref[...] = jnp.sum(jnp.where(row == lane_of((C, C)), piece[27], 0.0), axis=0, keepdims=True)
    finish(copies)


AUTO, HBM = pl.BlockSpec(), pl.BlockSpec(memory_space=pltpu.HBM)


def vmem(dims, kind):
    return pltpu.VMEM(dims, kind)


def sems(count):
    return pltpu.SemaphoreType.DMA((count,))


def shape(dims, kind):
    return jax.ShapeDtypeStruct(dims, kind)


def call(body, ins, outs, scratch, room, *operands):
    return pl.pallas_call(
        body,
        in_specs=ins,
        out_specs=[spec for spec, _ in outs],
        out_shape=[kind for _, kind in outs],
        scratch_shapes=scratch,
        compiler_params=pltpu.CompilerParams(vmem_limit_bytes=room),
    )(*operands)


def exchange(blocks, axis):
    return lax.all_to_all(blocks, axis, 0, 0, tiled=True)


FIELD = shape((YL, 128, NX), BF16)
SIDE = shape((YL, 32, NX), BF16)
FACE = shape((128, NX), BF16)
EDGE = shape((192, NX), BF16)
PAD = vmem((YL + 2, 192, NX), BF16)


def after(value, *others):
    return lax.optimization_barrier((value, *others))[0]


def z_halos(front, back):
    zlo = lax.ppermute(back, "gz", [(i, i + 1) for i in range(GZ - 1)])
    zhi = lax.ppermute(front, "gz", [(i + 1, i) for i in range(GZ - 1)])
    return zlo, zhi


def y_edges(first, last, zlo, zhi):
    return call(edges_kernel, [AUTO] * 4, [(AUTO, EDGE)] * 2, [], SMALL, first, last, zlo, zhi)


def y_halos(inner, outer):
    ahead = [(i, i + 1) for i in range(1, GY - 1, 2)]
    behind = [(i, i - 1) for i in range(2, GY, 2)]
    return (
        lax.ppermute(inner, "gy", [(i, i ^ 1) for i in range(GY)]),
        lax.ppermute(outer, "gy", ahead + behind),
    )


def conv(flip, own, halo, kernel, bias):
    return call(
        functools.partial(conv_kernel, flip),
        [HBM] * 7,
        [(HBM, FIELD)],
        [
            PAD, vmem((384, 576), BF16), vmem((YL, 128, NX), BF16),
            vmem((3, 3, C, 3 * C), BF16), vmem((1, C), F32), sems(7), sems(2),
        ],
        LARGE,
        own, *halo, kernel, bias,
    )[0]


def on_device(features, cotangent, spectral_weight, kernel_weight, channel_bias):
    own = features.reshape(YL, 128, NX)
    cot = cotangent.reshape(YL, 128, NX)
    weight = spectral_weight.reshape(64, 8192)
    bias = channel_bias.reshape(1, C)
    tx = jnp.asarray(x_forward_table())
    txi = jnp.asarray(x_inverse_table())
    table = jnp.asarray(joint_table())
    faces_out = [(HBM, SIDE)] * 2 + [(HBM, FACE)] * 2
    spectrum_out = (AUTO, shape((128, 128), F32))

    def lines_out(rows):
        return AUTO, shape((GY, rows, 128), BF16)

    def modes_out(rows):
        return AUTO, shape((GZ, rows, 128), BF16)

    both_rows = LINE_ROWS + 2 * GRAD_ROWS
    tail_rows = MODE_ROWS + TAIL_ROWS
    send, front, back, first, last = call(
        analyse_kernel,
        [HBM] * 2,
        [lines_out(2 * LINE_ROWS)] + faces_out,
        [vmem((YL, 128, NX), BF16), vmem((64, NX), BF16), sems(2), sems(4)],
        LARGE,
        own, tx,
    )
    recv = exchange(send, "gy")

    zlo, zhi = z_halos(front, back)
    (send,) = call(y_kernel, [AUTO] * 2, [modes_out(MODE_ROWS)], [], SMALL, recv, table)
    recv = exchange(send, "gz")
    send, spectrum = call(
        mix_kernel,
        [AUTO] * 3,
        [modes_out(4 * MODE_ROWS), spectrum_out],
        [vmem((256, 128), F32)],
        SMALL,
        recv, weight, table,
    )
    halo = (zlo, zhi, *y_halos(*y_edges(after(first, send), last, zlo, zhi)))
    recv = exchange(send, "gz")
    recv, *halo = lax.optimization_barrier((recv, *halo))
    (send,) = call(spread_kernel, [AUTO] * 2, [lines_out(LINE_ROWS)], [], SMALL, recv, table)
    local = conv(False, after(own, send), halo, kernel_weight, bias)
    recv = exchange(send, "gy")
    slope, front, back, first, last, send = call(
        slope_kernel,
        [HBM] * 10,
        [(HBM, FIELD)] + faces_out + [lines_out(both_rows)],
        [
            vmem((GY, LINE_ROWS, 128), BF16), vmem((YL, 128, NX), BF16), vmem((YL, 128, NX), BF16), PAD,
            vmem((192, NX), BF16), vmem((64, NX), BF16), vmem((512, 128), F32), vmem((YL, 128, NX), BF16),
            vmem((384, 576), F32), sems(10), sems(5),
        ],
        LARGE,
        recv, local, cot, own, *halo, txi, tx,
    )
    recv = exchange(send, "gy")

    zlo, zhi = z_halos(front, back)
    (send,) = call(
        y_back_kernel,
        [AUTO] * 2,
        [modes_out(tail_rows)],
        [vmem((GRAD_ROWS, 128), F32), vmem((GZ * TAIL_ROWS, 128), F32)],
        SMALL,
        recv, table,
    )
    recv = exchange(send, "gz")
    send, back = call(
        adjoint_kernel,
        [AUTO] * 3,
        [modes_out(4 * MODE_ROWS), spectrum_out],
        [vmem((256, 128), F32)],
        SMALL,
        recv, weight, table,
    )
    halo = (zlo, zhi, *y_halos(*y_edges(after(first, send), last, zlo, zhi)))
    recv = exchange(send, "gz")
    (grad_spectral,) = call(
        outer_kernel,
        [AUTO] * 2,
        [(HBM, shape((64, 8192), F32))],
        [vmem((64, 8192), F32), sems(KXL)],
        MEDIUM,
        after(spectrum, send), back,
    )
    recv, grad_spectral, *halo = lax.optimization_barrier((recv, grad_spectral, *halo))
    (send,) = call(
        spread_back_kernel,
        [AUTO] * 2,
        [lines_out(both_rows)],
        [vmem((GZ * TAIL_ROWS, 128), F32), vmem((2 * GRAD_ROWS, 128), F32)],
        SMALL,
        recv, table,
    )
    recv = exchange(send, "gy")
    conv_field = conv(True, after(slope, send), halo, kernel_weight, bias)
    grad_field, grad_kernel, grad_bias = call(
        final_kernel,
        [HBM] * 3,
        [(HBM, FIELD), (AUTO, shape((3, 3, C, 3 * C), F32)), (AUTO, shape((1, C), F32))],
        [
            vmem((GY, both_rows, 128), BF16), vmem((YL, 128, NX), BF16), vmem((192, NX), BF16),
            vmem((512, 128), F32), vmem((YL, 128, NX), BF16), sems(3), sems(2),
        ],
        MEDIUM,
        recv, conv_field, txi,
    )
    return (
        grad_field.reshape(features.shape),
        grad_spectral.reshape(spectral_weight.shape),
        grad_kernel,
        grad_bias.reshape(C),
    )


def solution(mesh):
    return jax.shard_map(
        on_device,
        mesh=mesh,
        in_specs=(
            P("gy", "gz", None, None),
            P("gy", "gz", None, None),
            P("gz", None, "gy"),
            P(),
            P(),
        ),
        out_specs=(P("gy", "gz", None, None), P("gz", None, "gy"), P(), P()),
        check_vma=False,
    )
```

```python
import functools
import math

import jax
import jax.numpy as jnp
import ml_dtypes
import numpy as np
from jax import lax
from jax.experimental import pallas as pl
from jax.experimental.pallas import tpu as pltpu
from jax.sharding import PartitionSpec as P

NX, NY, NZ = 512, 64, 64
C = 32
GY, GZ = 8, 16
YL, ZL = 8, 4
KXL = 4
LINE_ROWS = 64
MODE_ROWS = 16
GRAD_ROWS = 32
TAIL_ROWS = 8
SCALE = 1.0 / math.sqrt(NX * NY * NZ)
F32, BF16 = jnp.float32, jnp.bfloat16
LARGE = 60 * 1024 * 1024
MEDIUM = 48 * 1024 * 1024
SMALL = 16 * 1024 * 1024


def freqs(count, length):
    index = np.arange(count)
    return np.where(index < count // 2, index, length - count + index)


def angle(a, b, length):
    return 2.0 * math.pi / length * ((a[:, None] * b[None, :]) % length)


def split_np(table):
    high = table.astype(ml_dtypes.bfloat16)
    low = (table - high.astype(np.float64)).astype(ml_dtypes.bfloat16)
    return high, low


def x_forward_table():
    turn = angle(np.arange(32), np.arange(NX), NX)
    both = np.stack([np.cos(turn), -np.sin(turn)], 0).reshape(2, GY, KXL, NX)
    return both.transpose(1, 0, 2, 3).reshape(64, NX).astype(ml_dtypes.bfloat16)


def x_inverse_table():
    turn = angle(np.arange(32), np.arange(NX), NX)
    both = np.stack([np.cos(turn), -np.sin(turn)], 1).reshape(64, NX)
    high, low = split_np(both)
    return np.concatenate([high, low, high], 0)


def rotation(turn, sign):
    cos, sin = np.cos(turn), sign * np.sin(turn)
    return np.stack([np.stack([cos, -sin], -1), np.stack([sin, cos], -1)], 1)


def y_forward_table():
    turn = angle(freqs(32, NY), np.arange(NY), NY)
    table = rotation(turn, -1.0).reshape(GZ, 2, 2, NY, 2)
    full = np.einsum("gkpyq,ab->gakpyqb", table, np.eye(KXL)).reshape(256, 512)
    return full


def z_forward_table():
    turn = angle(freqs(32, NZ), np.arange(NZ), NZ)
    table = SCALE * rotation(turn, -1.0).reshape(32, 2, GZ, ZL, 2)
    full = np.einsum("kpgzq,ab->pakzbqg", table, np.eye(2)).reshape(128, 256)
    return full


def z_inverse_table():
    turn = angle(np.arange(NZ), freqs(32, NZ), NZ)
    table = SCALE * rotation(turn, 1.0).reshape(GZ, ZL, 2, 32, 2)
    full = np.einsum("gzpkq,ab->gapzqbk", table, np.eye(2)).reshape(256, 128)
    return full


def y_inverse_table():
    turn = angle(np.arange(NY), freqs(32, NY), NY)
    table = rotation(turn, 1.0).reshape(GY, YL, 2, GZ, 2, 2)
    full = np.einsum("dypgkq,ab->dapygkqb", table, np.eye(ZL)).reshape(512, 256)
    return full


def side_by_side(table):
    return np.concatenate(split_np(table), 1)


def joint_table():
    z_inverse = side_by_side(z_inverse_table())
    return np.concatenate(
        [
            *split_np(y_forward_table()),
            side_by_side(y_inverse_table()),
            side_by_side(z_forward_table()),
            np.concatenate([z_inverse, np.zeros_like(z_inverse)], 1),
        ],
        0,
    )


Y_INVERSE, Z_FORWARD, Z_INVERSE = 512, 1024, 1152


def split(value):
    high = value.astype(BF16)
    return high, (value - high.astype(F32)).astype(BF16)


def dot(a, b):
    return jnp.dot(a, b, preferred_element_type=F32)


def dot_nt(a, b):
    return lax.dot_general(a, b, (((1,), (1,)), ((), ())), preferred_element_type=F32)


def dot_tn(a, b):
    return lax.dot_general(a, b, (((0,), (0,)), ((), ())), preferred_element_type=F32)


def lane_of(shape):
    return lax.broadcasted_iota(jnp.int32, shape, len(shape) - 1)


def swap_blocks(parts):
    lane = lane_of(parts[0].shape)
    half = lane < 64
    p0, p1, p2, p3 = parts
    q0 = jnp.where(half, p0, pltpu.roll(p2, 64, 1))
    q2 = jnp.where(half, pltpu.roll(p0, 64, 1), p2)
    q1 = jnp.where(half, p1, pltpu.roll(p3, 64, 1))
    q3 = jnp.where(half, pltpu.roll(p1, 64, 1), p3)
    even = (lane & 32) == 0
    out = []
    for lo, hi in ((q0, q1), (q2, q3)):
        out.append(jnp.where(even, lo, pltpu.roll(hi, 32, 1)))
        out.append(jnp.where(even, pltpu.roll(lo, 96, 1), hi))
    return out


def pack_lines(lines, send_ref):
    for g in range(GY):
        block = jnp.concatenate([line[g * 8 : g * 8 + 8] for line in lines], 0)
        send_ref[g, 0:LINE_ROWS] = block.astype(BF16)


def collect_spectrum(recv_ref, table_ref, rows_ref):
    rows_ref[...] = recv_ref[:, 0:MODE_ROWS].astype(F32).reshape(256, 128)
    turned = []
    for j in range(4):
        turned.append(
            swap_blocks([rows_ref[pl.ds(k * 4 + j, GZ, stride=16), :] for k in range(KXL)])
        )
    joined = jnp.concatenate([turned[j][z] for z in range(ZL) for j in range(4)], 0).astype(BF16)
    rows = slice(Z_FORWARD, Z_FORWARD + 128)
    return dot(table_ref[rows, 0:256], joined) + dot(table_ref[rows, 256:512], joined)


def z_inverse(modes, table_ref):
    high, low = split(modes)
    rows = slice(Z_INVERSE, Z_INVERSE + 256)
    table_high, table_low = table_ref[rows, 0:128], table_ref[rows, 128:256]
    return dot(table_high, high) + dot(table_low, high) + dot(table_high, low)


def gain_lanes():
    lane = lane_of((128, 128))
    first = jnp.logical_and(lane < 32, lax.axis_index("gy") == 0)
    return jnp.where(first, 1.0, 2.0).astype(F32)


def repeat_matrix():
    row = lax.broadcasted_iota(jnp.int32, (64, 1024), 0) & 31
    return jnp.where(row == lane_of((64, 1024)) // 32, 1.0, 0.0).astype(BF16)


def spread(spectrum, k, matrix):
    high, low = split(spectrum[:, k * 32 : k * 32 + 32])
    return dot(jnp.concatenate([high, low], 1), matrix)


def fold_tiles(value):
    total = value[:, 0:128]
    for t in range(1, 8):
        total = total + value[:, t * 128 : t * 128 + 128]
    total = total + pltpu.roll(total, 64, 1)
    return total + pltpu.roll(total, 32, 1)


def place_fields(recv_ref, field_ref):
    for g in range(GY):
        block = recv_ref[g, 0:LINE_ROWS].astype(F32)
        turned = swap_blocks([block[z * 16 : z * 16 + 16] for z in range(ZL)])
        for k in range(KXL):
            for part in range(2):
                field_ref[pl.ds((g * 4 + k) * 2 + part, YL, stride=64), :] = turned[k][
                    part * 8 : part * 8 + 8
                ]


def x_inverse(field, table):
    high, low = split(field)
    return dot_tn(jnp.concatenate([high, high, low], 0), table)


def shift_right(value):
    return jnp.where(lane_of(value.shape) == 0, 0.0, pltpu.roll(value, 1, 1))


def shift_left(value):
    return jnp.where(lane_of(value.shape) == NX - 1, 0.0, pltpu.roll(value, NX - 1, 1))


def begin(copies, sems):
    started = [pltpu.make_async_copy(src, dst, sems.at[n]) for n, (src, dst) in enumerate(copies)]
    for copy in started:
        copy.start()
    return started


def finish(copies):
    for copy in copies:
        copy.wait()


def face_copies(field, front_ref, back_ref, first_ref, last_ref):
    return [
        (field.at[:, 0:32], front_ref),
        (field.at[:, 96:128], back_ref),
        (field.at[0], first_ref),
        (field.at[YL - 1], last_ref),
    ]


def analyse_kernel(own_ref, tx_hbm, send_ref, front_ref, back_ref, first_ref, last_ref, field, tx, in_sems, out_sems):
    finish(begin([(tx_hbm, tx), (own_ref, field)], in_sems))
    faces = begin(face_copies(field, front_ref, back_ref, first_ref, last_ref), out_sems)
    lines = [dot_nt(tx[...], field[y]) for y in range(YL)]
    pack_lines(lines, send_ref)
    send_ref[:, LINE_ROWS:] = jnp.zeros((GY, LINE_ROWS, 128), BF16)
    finish(faces)


def y_kernel(recv_ref, table_ref, send_ref):
    lines = recv_ref[:, 0:LINE_ROWS].reshape(512, 128)
    out = dot(table_ref[0:256], lines) + dot(table_ref[256:512], lines)
    send_ref[:, 0:MODE_ROWS] = out.astype(BF16).reshape(GZ, MODE_ROWS, 128)


def y_back_kernel(recv_ref, table_ref, send_ref, sums_ref, tail_ref):
    y_kernel(recv_ref, table_ref, send_ref)
    total = jnp.zeros((2 * GRAD_ROWS, 128), F32)
    for g in range(GY):
        total = total + recv_ref[g, LINE_ROWS : LINE_ROWS + 2 * GRAD_ROWS].astype(F32)
    sums_ref[...] = total[0:GRAD_ROWS] + total[GRAD_ROWS : 2 * GRAD_ROWS]
    tail_ref[...] = jnp.zeros_like(tail_ref)
    for r in range(2):
        rows = sums_ref[pl.ds(r, GZ, stride=2), :]
        high = rows.astype(BF16).astype(F32)
        tail_ref[pl.ds(r, GZ, stride=TAIL_ROWS), :] = high
        tail_ref[pl.ds(r + 2, GZ, stride=TAIL_ROWS), :] = rows - high
    tail = tail_ref[...].reshape(GZ, TAIL_ROWS, 128)
    send_ref[:, MODE_ROWS : MODE_ROWS + TAIL_ROWS] = tail.astype(BF16)


def spread_kernel(recv_ref, table_ref, send_ref):
    modes = recv_ref[:, 0:MODE_ROWS].reshape(256, 128)
    rows = slice(Y_INVERSE, Y_INVERSE + 512)
    out = dot(table_ref[rows, 0:256], modes) + dot(table_ref[rows, 256:512], modes)
    send_ref[:, 0:LINE_ROWS] = out.astype(BF16).reshape(GY, LINE_ROWS, 128)


def spread_back_kernel(recv_ref, table_ref, send_ref, tail_ref, both_ref):
    spread_kernel(recv_ref, table_ref, send_ref)
    tail = recv_ref[:, MODE_ROWS : MODE_ROWS + TAIL_ROWS].astype(F32)
    tail_ref[...] = tail.reshape(GZ * TAIL_ROWS, 128)
    for r in range(2):
        both_ref[pl.ds(r, GZ, stride=2), :] = tail_ref[pl.ds(r, GZ, stride=TAIL_ROWS), :]
        both_ref[pl.ds(GRAD_ROWS + r, GZ, stride=2), :] = tail_ref[pl.ds(r + 2, GZ, stride=TAIL_ROWS), :]
    both = both_ref[...].astype(BF16)
    for g in range(GY):
        send_ref[g, LINE_ROWS : LINE_ROWS + 2 * GRAD_ROWS] = both


def own_core():
    return lax.rem(lax.axis_index("gy"), 2)


def edges_kernel(own_first_ref, own_last_ref, zlo_ref, zhi_ref, inner_ref, outer_ref):
    first, last = [
        jnp.concatenate([zlo_ref[y], own[...], zhi_ref[y]], 0)
        for y, own in ((0, own_first_ref), (YL - 1, own_last_ref))
    ]
    even = own_core() == 0
    inner_ref[...] = jnp.where(even, last, first)
    outer_ref[...] = jnp.where(even, first, last)


def pad_copies(pad, own_ref, zlo_ref, zhi_ref, inner_ref, outer_ref):
    return [
        (own_ref, pad.at[1:9, 32:160]),
        (zlo_ref, pad.at[1:9, 0:32]),
        (zhi_ref, pad.at[1:9, 160:192]),
        (inner_ref, pad.at[(1 - own_core()) * (YL + 1)]),
        (outer_ref, pad.at[own_core() * (YL + 1)]),
    ]


def mix_kernel(recv_ref, weight_ref, table_ref, send_ref, spec_ref, rows_ref):
    spectrum = collect_spectrum(recv_ref, table_ref, rows_ref)
    spec_ref[...] = spectrum
    matrix = repeat_matrix()
    lane = lane_of((64, 128)) // 32
    real = jnp.zeros((64, 128), F32)
    imag = jnp.zeros((64, 128), F32)
    for k in range(KXL):
        wide = spread(spectrum, k, matrix)
        w_re = weight_ref[:, k * 2048 : k * 2048 + 1024].astype(F32)
        w_im = weight_ref[:, k * 2048 + 1024 : k * 2048 + 2048].astype(F32)
        s_re, s_im = wide[0:64], wide[64:128]
        real = jnp.where(lane == k, fold_tiles(s_re * w_re - s_im * w_im), real)
        imag = jnp.where(lane == k, fold_tiles(s_re * w_im + s_im * w_re), imag)
    modes = jnp.concatenate([real, imag], 0) * gain_lanes()
    send_ref[:, MODE_ROWS:] = jnp.zeros((GZ, 3 * MODE_ROWS, 128), BF16)
    send_ref[:, 0:MODE_ROWS] = z_inverse(modes, table_ref).astype(BF16).reshape(GZ, MODE_ROWS, 128)


def build_taps(kernel_ref, taps, flip):
    row = lax.broadcasted_iota(jnp.int32, (C, C), 0)
    eye = jnp.where(row == lane_of((C, C)), 1.0, 0.0).astype(BF16)
    tap = {}
    for dy in range(3):
        for dz in range(3):
            if flip:
                turned = dot_tn(kernel_ref[2 - dy, 2 - dz], eye)
                for dx in range(3):
                    tap[dx, dy, dz] = turned[(2 - dx) * C : (2 - dx) * C + C]
            else:
                whole = kernel_ref[dy, dz].astype(F32)
                for dx in range(3):
                    tap[dx, dy, dz] = whole[:, dx * C : dx * C + C]
    for dx in range(3):
        parts = []
        for dy in range(3):
            parts += [tap[dx, dy, dz] for dz in range(3)] + [jnp.zeros((C, 96), F32)]
        base = jnp.concatenate(parts + [jnp.zeros((C, 64), F32)], 1)
        for z in range(ZL):
            row = (dx * ZL + z) * C
            moved = pltpu.roll(base, z * C, 1) if z else base
            taps[row : row + C, :] = moved[:, 0:576].astype(BF16)


def conv_kernel(
    flip, own_ref, zlo_ref, zhi_ref, inner_ref, outer_ref, kernel_hbm, bias_hbm, out_ref,
    pad, taps, buffer, kernel_ref, bias_ref, in_sems, out_sems,
):
    fetched = begin(
        [(kernel_hbm, kernel_ref), (bias_hbm, bias_ref)]
        + pad_copies(pad, own_ref, zlo_ref, zhi_ref, inner_ref, outer_ref),
        in_sems,
    )
    finish(fetched[0:2])
    padded = fetched[2:]
    build_taps(kernel_ref, taps, flip)
    if not flip:
        row = lax.broadcasted_iota(jnp.int32, (128, C), 0) & 31
        picked = jnp.where(row == lane_of((128, C)), bias_ref[...], 0.0)
        bias = jnp.sum(picked, axis=1, keepdims=True)
    finish(padded)
    copies = []
    for y in range(YL):
        wide = dot(taps[...], pad[y : y + 3].reshape(576, NX))
        total = wide[128:256] + shift_right(wide[0:128]) + shift_left(wide[256:384])
        buffer[y] = (total if flip else total + bias).astype(BF16)
        if y % 4 == 3:
            half = slice(y - 3, y + 1)
            copies += begin([(buffer.at[half], out_ref.at[half])], out_sems.at[y // 4 : y // 4 + 1])
    finish(copies)


def slope_kernel(
    recv_ref, local_ref, cot_ref, own_ref, zlo_ref, zhi_ref, inner_ref, outer_ref, txi_hbm, tx_hbm,
    slope_ref, front_ref, back_ref, first_ref, last_ref, send_ref,
    recv, local, cot, pad, txi, tx, field_ref, slopes, sums_ref, in_sems, out_sems,
):
    fetched = begin(
        [(recv_ref, recv), (txi_hbm, txi), (tx_hbm, tx), (local_ref, local), (cot_ref, cot)]
        + pad_copies(pad, own_ref, zlo_ref, zhi_ref, inner_ref, outer_ref),
        in_sems,
    )
    fetched[0].wait()
    place_fields(recv, field_ref)
    finish(fetched[1:5])
    root = math.sqrt(2.0 / math.pi)
    lines = []
    for y in range(YL):
        pre = x_inverse(field_ref[y * 64 : y * 64 + 64], txi[...]) + local[y].astype(F32)
        square = pre * pre
        bent = jnp.tanh(root * pre * (1.0 + 0.044715 * square))
        rate = 0.5 * (1.0 + bent) + 0.5 * root * pre * (1.0 - bent * bent) * (
            1.0 + 3.0 * 0.044715 * square
        )
        slope = (cot[y].astype(F32) * rate).astype(BF16)
        slopes[y] = slope
        lines.append(dot_nt(tx[...], slope))
    copies = begin(
        face_copies(slopes, front_ref, back_ref, first_ref, last_ref) + [(slopes, slope_ref)], out_sems
    )
    pack_lines(lines, send_ref)
    finish(fetched[5:])
    bias = jnp.zeros((128, 1), F32)
    for start in range(0, YL, 4):
        left, right = [], []
        for y in range(start, start + 4):
            slope = slopes[y]
            wide = slope.astype(F32)
            bias = bias + jnp.sum(wide, axis=1, keepdims=True)
            left.append(
                jnp.concatenate([shift_left(wide).astype(BF16), slope, shift_right(wide).astype(BF16)], 0)
            )
            right.append(pad[y : y + 3].reshape(576, NX))
        part = dot_nt(jnp.concatenate(left, 1), jnp.concatenate(right, 1))
        sums_ref[...] = part if start == 0 else sums_ref[...] + part
    bias32 = bias[0:32] + bias[32:64] + bias[64:96] + bias[96:128]
    pieces = []
    for dx in range(3):
        for dy in range(3):
            total = jnp.zeros((C, 96), F32)
            for z in range(ZL):
                row = (dx * ZL + z) * C
                col = dy * 192 + z * C
                total = total + sums_ref[row : row + C, col : col + 96]
            pieces += [total[:, dz * C : dz * C + C] for dz in range(3)]
    pieces.append(jnp.broadcast_to(bias32, (C, C)))
    for g in range(GY):
        if g < 7:
            rows = jnp.concatenate(pieces[4 * g : 4 * g + 4], 1)
        else:
            rows = jnp.zeros((C, 128), F32)
        high, low = split(rows)
        send_ref[g, LINE_ROWS : LINE_ROWS + GRAD_ROWS] = high
        send_ref[g, LINE_ROWS + GRAD_ROWS : LINE_ROWS + 2 * GRAD_ROWS] = low
    finish(copies)


def adjoint_kernel(recv_ref, weight_ref, table_ref, send_ref, spec_ref, rows_ref):
    spectrum = collect_spectrum(recv_ref, table_ref, rows_ref)
    spec_ref[...] = spectrum
    row = lax.broadcasted_iota(jnp.int32, (1024, 128), 0) // 32
    lane = lane_of((1024, 128))
    gather = []
    for k in range(KXL):
        w_re = weight_ref[:, k * 2048 : k * 2048 + 1024].astype(F32)
        w_im = weight_ref[:, k * 2048 + 1024 : k * 2048 + 2048].astype(F32)
        own = spectrum[:, k * 32 : k * 32 + 32]
        four = jnp.concatenate([own] * 4, 1)
        wide = jnp.concatenate([four] * 8, 1)
        b_re, b_im = wide[0:64], wide[64:128]
        both = jnp.concatenate([b_re * w_re + b_im * w_im, b_im * w_re - b_re * w_im], 0)
        matrix = jnp.where(row + k * 32 == lane, 1.0, 0.0).astype(BF16)
        high, low = split(both)
        gather.append(dot(high, matrix) + dot(low, matrix))
    modes = (gather[0] + gather[1] + gather[2] + gather[3]) * gain_lanes()
    send_ref[:, MODE_ROWS:] = jnp.zeros((GZ, 3 * MODE_ROWS, 128), BF16)
    block = z_inverse(modes, table_ref).astype(BF16)
    send_ref[:, 0:MODE_ROWS] = block.reshape(GZ, MODE_ROWS, 128)
    total = jnp.sum(recv_ref[:, MODE_ROWS : MODE_ROWS + TAIL_ROWS].astype(F32), axis=0)
    total = total + pltpu.roll(total, TAIL_ROWS - 2, 0)
    high = total.astype(BF16).astype(F32)
    part = lax.broadcasted_iota(jnp.int32, (TAIL_ROWS, 128), 0)
    low = jnp.where(part < 4, pltpu.roll(total - high, 2, 0), 0.0)
    tail = jnp.where(part < 2, high, low).astype(BF16)
    send_ref[:, MODE_ROWS : MODE_ROWS + TAIL_ROWS] = jnp.broadcast_to(tail[None], (GZ, TAIL_ROWS, 128))


def outer_kernel(spec_ref, back_ref, out_hbm, out_ref, sems):
    copies = []
    matrix = repeat_matrix()
    gain = gain_lanes()
    spectrum = spec_ref[...]
    back = back_ref[...] * gain
    for k in range(KXL):
        wide = spread(spectrum, k, matrix)
        s_re, s_im = wide[0:64], wide[64:128]
        own = back[:, k * 32 : k * 32 + 32]
        four = jnp.concatenate([own] * 4, 1)
        tiled = jnp.concatenate([four] * 8, 1)
        b_re, b_im = tiled[0:64], tiled[64:128]
        out_ref[:, k * 2048 : k * 2048 + 1024] = s_re * b_re + s_im * b_im
        out_ref[:, k * 2048 + 1024 : k * 2048 + 2048] = s_re * b_im - s_im * b_re
        part = slice(k * 2048, k * 2048 + 2048)
        copies += begin([(out_ref.at[:, part], out_hbm.at[:, part])], sems.at[k : k + 1])
    finish(copies)


def final_kernel(
    recv_ref, conv_ref, txi_hbm, grad_ref, kernel_ref, bias_ref,
    recv, conv, txi, field_ref, grads, in_sems, out_sems,
):
    fetched = begin([(recv_ref, recv), (txi_hbm, txi), (conv_ref, conv)], in_sems)
    fetched[0].wait()
    place_fields(recv, field_ref)
    finish(fetched[1:])
    copies = []
    for y in range(YL):
        back = x_inverse(field_ref[y * 64 : y * 64 + 64], txi[...])
        grads[y] = (back + conv[y].astype(F32)).astype(BF16)
        if y % 4 == 3:
            half = slice(y - 3, y + 1)
            copies += begin([(grads.at[half], grad_ref.at[half])], out_sems.at[y // 4 : y // 4 + 1])
    piece = []
    for g in range(7):
        high = recv[g, LINE_ROWS : LINE_ROWS + GRAD_ROWS].astype(F32)
        low = recv[g, LINE_ROWS + GRAD_ROWS : LINE_ROWS + 2 * GRAD_ROWS].astype(F32)
        rows = SCALE * (high + low)
        piece += [rows[:, j * C : j * C + C] for j in range(4)]
    for dy in range(3):
        for dz in range(3):
            kernel_ref[dy, dz] = jnp.concatenate([piece[dx * 9 + dy * 3 + dz] for dx in range(3)], 1)
    row = lax.broadcasted_iota(jnp.int32, (C, C), 0)
    bias_ref[...] = jnp.sum(jnp.where(row == lane_of((C, C)), piece[27], 0.0), axis=0, keepdims=True)
    finish(copies)


AUTO, HBM = pl.BlockSpec(), pl.BlockSpec(memory_space=pltpu.HBM)


def vmem(dims, kind):
    return pltpu.VMEM(dims, kind)


def sems(count):
    return pltpu.SemaphoreType.DMA((count,))


def shape(dims, kind):
    return jax.ShapeDtypeStruct(dims, kind)


def call(body, ins, outs, scratch, room, *operands):
    return pl.pallas_call(
        body,
        in_specs=ins,
        out_specs=[spec for spec, _ in outs],
        out_shape=[kind for _, kind in outs],
        scratch_shapes=scratch,
        compiler_params=pltpu.CompilerParams(vmem_limit_bytes=room),
    )(*operands)


def exchange(blocks, axis):
    return lax.all_to_all(blocks, axis, 0, 0, tiled=True)


FIELD = shape((YL, 128, NX), BF16)
SIDE = shape((YL, 32, NX), BF16)
FACE = shape((128, NX), BF16)
EDGE = shape((192, NX), BF16)
PAD = vmem((YL + 2, 192, NX), BF16)


def after(value, *others):
    return lax.optimization_barrier((value, *others))[0]


def z_halos(front, back):
    zlo = lax.ppermute(back, "gz", [(i, i + 1) for i in range(GZ - 1)])
    zhi = lax.ppermute(front, "gz", [(i + 1, i) for i in range(GZ - 1)])
    return zlo, zhi


def y_edges(first, last, zlo, zhi):
    return call(edges_kernel, [AUTO] * 4, [(AUTO, EDGE)] * 2, [], SMALL, first, last, zlo, zhi)


def y_halos(inner, outer):
    ahead = [(i, i + 1) for i in range(1, GY - 1, 2)]
    behind = [(i, i - 1) for i in range(2, GY, 2)]
    outer = lax.ppermute(outer, "gy", ahead + behind)
    inner = lax.ppermute(inner, "gy", [(i, i ^ 1) for i in range(GY)])
    return inner, outer


def conv(flip, own, halo, kernel, bias):
    return call(
        functools.partial(conv_kernel, flip),
        [HBM] * 7,
        [(HBM, FIELD)],
        [
            PAD, vmem((384, 576), BF16), vmem((YL, 128, NX), BF16),
            vmem((3, 3, C, 3 * C), BF16), vmem((1, C), F32), sems(7), sems(2),
        ],
        LARGE,
        own, *halo, kernel, bias,
    )[0]


def on_device(features, cotangent, spectral_weight, kernel_weight, channel_bias):
    own = features.reshape(YL, 128, NX)
    cot = cotangent.reshape(YL, 128, NX)
    weight = spectral_weight.reshape(64, 8192)
    bias = channel_bias.reshape(1, C)
    tx = jnp.asarray(x_forward_table())
    txi = jnp.asarray(x_inverse_table())
    table = jnp.asarray(joint_table())
    faces_out = [(HBM, SIDE)] * 2 + [(HBM, FACE)] * 2
    spectrum_out = (AUTO, shape((128, 128), F32))

    def lines_out(rows):
        return AUTO, shape((GY, rows, 128), BF16)

    def modes_out(rows):
        return AUTO, shape((GZ, rows, 128), BF16)

    both_rows = LINE_ROWS + 2 * GRAD_ROWS
    tail_rows = MODE_ROWS + TAIL_ROWS
    send, front, back, first, last = call(
        analyse_kernel,
        [HBM] * 2,
        [lines_out(2 * LINE_ROWS)] + faces_out,
        [vmem((YL, 128, NX), BF16), vmem((64, NX), BF16), sems(2), sems(4)],
        LARGE,
        own, tx,
    )
    recv = exchange(send, "gy")

    zlo, zhi = z_halos(front, back)
    (send,) = call(y_kernel, [AUTO] * 2, [modes_out(MODE_ROWS)], [], SMALL, recv, table)
    recv = exchange(send, "gz")
    send, spectrum = call(
        mix_kernel,
        [AUTO] * 3,
        [modes_out(4 * MODE_ROWS), spectrum_out],
        [vmem((256, 128), F32)],
        SMALL,
        recv, weight, table,
    )
    halo = (zlo, zhi, *y_halos(*y_edges(after(first, send), last, zlo, zhi)))
    recv = exchange(send, "gz")
    recv, inner = lax.optimization_barrier((recv, halo[2]))
    halo = (zlo, zhi, inner, halo[3])
    (send,) = call(spread_kernel, [AUTO] * 2, [lines_out(LINE_ROWS)], [], SMALL, recv, table)
    local = conv(False, after(own, send), halo, kernel_weight, bias)
    recv = exchange(send, "gy")
    slope, front, back, first, last, send = call(
        slope_kernel,
        [HBM] * 10,
        [(HBM, FIELD)] + faces_out + [lines_out(both_rows)],
        [
            vmem((GY, LINE_ROWS, 128), BF16), vmem((YL, 128, NX), BF16), vmem((YL, 128, NX), BF16), PAD,
            vmem((192, NX), BF16), vmem((64, NX), BF16), vmem((512, 128), F32), vmem((YL, 128, NX), BF16),
            vmem((384, 576), F32), sems(10), sems(5),
        ],
        LARGE,
        recv, local, cot, own, *halo, txi, tx,
    )
    recv = exchange(send, "gy")

    zlo, zhi = z_halos(front, back)
    (send,) = call(
        y_back_kernel,
        [AUTO] * 2,
        [modes_out(tail_rows)],
        [vmem((GRAD_ROWS, 128), F32), vmem((GZ * TAIL_ROWS, 128), F32)],
        SMALL,
        recv, table,
    )
    recv = exchange(send, "gz")
    send, back = call(
        adjoint_kernel,
        [AUTO] * 3,
        [modes_out(4 * MODE_ROWS), spectrum_out],
        [vmem((256, 128), F32)],
        SMALL,
        recv, weight, table,
    )
    halo = (zlo, zhi, *y_halos(*y_edges(after(first, send), last, zlo, zhi)))
    recv = exchange(send, "gz")
    (grad_spectral,) = call(
        outer_kernel,
        [AUTO] * 2,
        [(HBM, shape((64, 8192), F32))],
        [vmem((64, 8192), F32), sems(KXL)],
        MEDIUM,
        after(spectrum, send), back,
    )
    recv, grad_spectral, *halo = lax.optimization_barrier((recv, grad_spectral, *halo))
    (send,) = call(
        spread_back_kernel,
        [AUTO] * 2,
        [lines_out(both_rows)],
        [vmem((GZ * TAIL_ROWS, 128), F32), vmem((2 * GRAD_ROWS, 128), F32)],
        SMALL,
        recv, table,
    )
    recv = exchange(send, "gy")
    conv_field = conv(True, after(slope, send), halo, kernel_weight, bias)
    grad_field, grad_kernel, grad_bias = call(
        final_kernel,
        [HBM] * 3,
        [(HBM, FIELD), (AUTO, shape((3, 3, C, 3 * C), F32)), (AUTO, shape((1, C), F32))],
        [
            vmem((GY, both_rows, 128), BF16), vmem((YL, 128, NX), BF16), vmem((192, NX), BF16),
            vmem((512, 128), F32), vmem((YL, 128, NX), BF16), sems(3), sems(2),
        ],
        MEDIUM,
        recv, conv_field, txi,
    )
    return (
        grad_field.reshape(features.shape),
        grad_spectral.reshape(spectral_weight.shape),
        grad_kernel,
        grad_bias.reshape(C),
    )


def solution(mesh):
    return jax.shard_map(
        on_device,
        mesh=mesh,
        in_specs=(
            P("gy", "gz", None, None),
            P("gy", "gz", None, None),
            P("gz", None, "gy"),
            P(),
            P(),
        ),
        out_specs=(P("gy", "gz", None, None), P("gz", None, "gy"), P(), P()),
        check_vma=False,
    )
```

```python
import functools
import math

import jax
import jax.numpy as jnp
import ml_dtypes
import numpy as np
from jax import lax
from jax.experimental import pallas as pl
from jax.experimental.pallas import tpu as pltpu
from jax.sharding import PartitionSpec as P

NX, NY, NZ = 512, 64, 64
C = 32
GY, GZ = 8, 16
YL, ZL = 8, 4
KXL = 4
LINE_ROWS = 64
MODE_ROWS = 16
GRAD_ROWS = 32
TAIL_ROWS = 8
SCALE = 1.0 / math.sqrt(NX * NY * NZ)
F32, BF16 = jnp.float32, jnp.bfloat16
LARGE = 60 * 1024 * 1024
MEDIUM = 48 * 1024 * 1024
SMALL = 16 * 1024 * 1024


def freqs(count, length):
    index = np.arange(count)
    return np.where(index < count // 2, index, length - count + index)


def angle(a, b, length):
    return 2.0 * math.pi / length * ((a[:, None] * b[None, :]) % length)


def split_np(table):
    high = table.astype(ml_dtypes.bfloat16)
    low = (table - high.astype(np.float64)).astype(ml_dtypes.bfloat16)
    return high, low


def x_forward_table():
    turn = angle(np.arange(32), np.arange(NX), NX)
    both = np.stack([np.cos(turn), -np.sin(turn)], 0).reshape(2, GY, KXL, NX)
    return both.transpose(1, 0, 2, 3).reshape(64, NX).astype(ml_dtypes.bfloat16)


def x_inverse_table():
    turn = angle(np.arange(32), np.arange(NX), NX)
    both = np.stack([np.cos(turn), -np.sin(turn)], 1).reshape(64, NX)
    high, low = split_np(both)
    return np.concatenate([high, low, high], 0)


def rotation(turn, sign):
    cos, sin = np.cos(turn), sign * np.sin(turn)
    return np.stack([np.stack([cos, -sin], -1), np.stack([sin, cos], -1)], 1)


def y_forward_table():
    turn = angle(freqs(32, NY), np.arange(NY), NY)
    table = rotation(turn, -1.0).reshape(GZ, 2, 2, NY, 2)
    full = np.einsum("gkpyq,ab->gakpyqb", table, np.eye(KXL)).reshape(256, 512)
    return full


def z_forward_table():
    turn = angle(freqs(32, NZ), np.arange(NZ), NZ)
    table = SCALE * rotation(turn, -1.0).reshape(32, 2, GZ, ZL, 2)
    full = np.einsum("kpgzq,ab->pakzbqg", table, np.eye(2)).reshape(128, 256)
    return full


def z_inverse_table():
    turn = angle(np.arange(NZ), freqs(32, NZ), NZ)
    table = SCALE * rotation(turn, 1.0).reshape(GZ, ZL, 2, 32, 2)
    full = np.einsum("gzpkq,ab->gapzqbk", table, np.eye(2)).reshape(256, 128)
    return full


def y_inverse_table():
    turn = angle(np.arange(NY), freqs(32, NY), NY)
    table = rotation(turn, 1.0).reshape(GY, YL, 2, GZ, 2, 2)
    full = np.einsum("dypgkq,ab->dapygkqb", table, np.eye(ZL)).reshape(512, 256)
    return full


def side_by_side(table):
    return np.concatenate(split_np(table), 1)


def joint_table():
    z_inverse = side_by_side(z_inverse_table())
    return np.concatenate(
        [
            *split_np(y_forward_table()),
            side_by_side(y_inverse_table()),
            side_by_side(z_forward_table()),
            np.concatenate([z_inverse, np.zeros_like(z_inverse)], 1),
        ],
        0,
    )


Y_INVERSE, Z_FORWARD, Z_INVERSE = 512, 1024, 1152


def split(value):
    high = value.astype(BF16)
    return high, (value - high.astype(F32)).astype(BF16)


def dot(a, b):
    return jnp.dot(a, b, preferred_element_type=F32)


def dot_nt(a, b):
    return lax.dot_general(a, b, (((1,), (1,)), ((), ())), preferred_element_type=F32)


def dot_tn(a, b):
    return lax.dot_general(a, b, (((0,), (0,)), ((), ())), preferred_element_type=F32)


def lane_of(shape):
    return lax.broadcasted_iota(jnp.int32, shape, len(shape) - 1)


def swap_blocks(parts):
    lane = lane_of(parts[0].shape)
    half = lane < 64
    p0, p1, p2, p3 = parts
    q0 = jnp.where(half, p0, pltpu.roll(p2, 64, 1))
    q2 = jnp.where(half, pltpu.roll(p0, 64, 1), p2)
    q1 = jnp.where(half, p1, pltpu.roll(p3, 64, 1))
    q3 = jnp.where(half, pltpu.roll(p1, 64, 1), p3)
    even = (lane & 32) == 0
    out = []
    for lo, hi in ((q0, q1), (q2, q3)):
        out.append(jnp.where(even, lo, pltpu.roll(hi, 32, 1)))
        out.append(jnp.where(even, pltpu.roll(lo, 96, 1), hi))
    return out


def pack_lines(lines, send_ref):
    for g in range(GY):
        block = jnp.concatenate([line[g * 8 : g * 8 + 8] for line in lines], 0)
        send_ref[g, 0:LINE_ROWS] = block.astype(BF16)


def collect_spectrum(recv_ref, table_ref, rows_ref):
    rows_ref[...] = recv_ref[:, 0:MODE_ROWS].astype(F32).reshape(256, 128)
    turned = []
    for j in range(4):
        turned.append(
            swap_blocks([rows_ref[pl.ds(k * 4 + j, GZ, stride=16), :] for k in range(KXL)])
        )
    joined = jnp.concatenate([turned[j][z] for z in range(ZL) for j in range(4)], 0).astype(BF16)
    rows = slice(Z_FORWARD, Z_FORWARD + 128)
    return dot(table_ref[rows, 0:256], joined) + dot(table_ref[rows, 256:512], joined)


def z_inverse(modes, table_ref):
    high, low = split(modes)
    rows = slice(Z_INVERSE, Z_INVERSE + 256)
    table_high, table_low = table_ref[rows, 0:128], table_ref[rows, 128:256]
    return dot(table_high, high) + dot(table_low, high) + dot(table_high, low)


def gain_lanes():
    lane = lane_of((128, 128))
    first = jnp.logical_and(lane < 32, lax.axis_index("gy") == 0)
    return jnp.where(first, 1.0, 2.0).astype(F32)


def repeat_matrix():
    row = lax.broadcasted_iota(jnp.int32, (64, 1024), 0) & 31
    return jnp.where(row == lane_of((64, 1024)) // 32, 1.0, 0.0).astype(BF16)


def spread(spectrum, k, matrix):
    high, low = split(spectrum[:, k * 32 : k * 32 + 32])
    return dot(jnp.concatenate([high, low], 1), matrix)


def fold_tiles(value):
    total = value[:, 0:128]
    for t in range(1, 8):
        total = total + value[:, t * 128 : t * 128 + 128]
    total = total + pltpu.roll(total, 64, 1)
    return total + pltpu.roll(total, 32, 1)


def place_fields(recv_ref, field_ref):
    for g in range(GY):
        block = recv_ref[g, 0:LINE_ROWS].astype(F32)
        turned = swap_blocks([block[z * 16 : z * 16 + 16] for z in range(ZL)])
        for k in range(KXL):
            for part in range(2):
                field_ref[pl.ds((g * 4 + k) * 2 + part, YL, stride=64), :] = turned[k][
                    part * 8 : part * 8 + 8
                ]


def x_inverse(field, table):
    high, low = split(field)
    return dot_tn(jnp.concatenate([high, high, low], 0), table)


def shift_right(value):
    return jnp.where(lane_of(value.shape) == 0, 0.0, pltpu.roll(value, 1, 1))


def shift_left(value):
    return jnp.where(lane_of(value.shape) == NX - 1, 0.0, pltpu.roll(value, NX - 1, 1))


def begin(copies, sems):
    started = [pltpu.make_async_copy(src, dst, sems.at[n]) for n, (src, dst) in enumerate(copies)]
    for copy in started:
        copy.start()
    return started


def finish(copies):
    for copy in copies:
        copy.wait()


def face_copies(field, front_ref, back_ref, first_ref, last_ref):
    return [
        (field.at[:, 0:32], front_ref),
        (field.at[:, 96:128], back_ref),
        (field.at[0], first_ref),
        (field.at[YL - 1], last_ref),
    ]


def analyse_kernel(own_ref, tx_hbm, send_ref, front_ref, back_ref, first_ref, last_ref, field, tx, in_sems, out_sems):
    finish(begin([(tx_hbm, tx), (own_ref, field)], in_sems))
    faces = begin(face_copies(field, front_ref, back_ref, first_ref, last_ref), out_sems)
    lines = [dot_nt(tx[...], field[y]) for y in range(YL)]
    pack_lines(lines, send_ref)
    send_ref[:, LINE_ROWS:] = jnp.zeros((GY, LINE_ROWS, 128), BF16)
    finish(faces)


def y_kernel(recv_ref, table_ref, send_ref):
    lines = recv_ref[:, 0:LINE_ROWS].reshape(512, 128)
    out = dot(table_ref[0:256], lines) + dot(table_ref[256:512], lines)
    send_ref[:, 0:MODE_ROWS] = out.astype(BF16).reshape(GZ, MODE_ROWS, 128)


def y_back_kernel(recv_ref, table_ref, send_ref, sums_ref, tail_ref):
    y_kernel(recv_ref, table_ref, send_ref)
    total = jnp.zeros((2 * GRAD_ROWS, 128), F32)
    for g in range(GY):
        total = total + recv_ref[g, LINE_ROWS : LINE_ROWS + 2 * GRAD_ROWS].astype(F32)
    sums_ref[...] = total[0:GRAD_ROWS] + total[GRAD_ROWS : 2 * GRAD_ROWS]
    tail_ref[...] = jnp.zeros_like(tail_ref)
    for r in range(2):
        rows = sums_ref[pl.ds(r, GZ, stride=2), :]
        high = rows.astype(BF16).astype(F32)
        tail_ref[pl.ds(r, GZ, stride=TAIL_ROWS), :] = high
        tail_ref[pl.ds(r + 2, GZ, stride=TAIL_ROWS), :] = rows - high
    tail = tail_ref[...].reshape(GZ, TAIL_ROWS, 128)
    send_ref[:, MODE_ROWS : MODE_ROWS + TAIL_ROWS] = tail.astype(BF16)


def spread_kernel(recv_ref, table_ref, send_ref):
    modes = recv_ref[:, 0:MODE_ROWS].reshape(256, 128)
    rows = slice(Y_INVERSE, Y_INVERSE + 512)
    out = dot(table_ref[rows, 0:256], modes) + dot(table_ref[rows, 256:512], modes)
    send_ref[:, 0:LINE_ROWS] = out.astype(BF16).reshape(GY, LINE_ROWS, 128)


def spread_back_kernel(recv_ref, table_ref, send_ref, tail_ref, both_ref):
    spread_kernel(recv_ref, table_ref, send_ref)
    tail = recv_ref[:, MODE_ROWS : MODE_ROWS + TAIL_ROWS].astype(F32)
    tail_ref[...] = tail.reshape(GZ * TAIL_ROWS, 128)
    for r in range(2):
        both_ref[pl.ds(r, GZ, stride=2), :] = tail_ref[pl.ds(r, GZ, stride=TAIL_ROWS), :]
        both_ref[pl.ds(GRAD_ROWS + r, GZ, stride=2), :] = tail_ref[pl.ds(r + 2, GZ, stride=TAIL_ROWS), :]
    both = both_ref[...].astype(BF16)
    for g in range(GY):
        send_ref[g, LINE_ROWS : LINE_ROWS + 2 * GRAD_ROWS] = both


def own_core():
    return lax.rem(lax.axis_index("gy"), 2)


def edges_kernel(own_first_ref, own_last_ref, zlo_ref, zhi_ref, inner_ref, outer_ref):
    first, last = [
        jnp.concatenate([zlo_ref[y], own[...], zhi_ref[y]], 0)
        for y, own in ((0, own_first_ref), (YL - 1, own_last_ref))
    ]
    even = own_core() == 0
    inner_ref[...] = jnp.where(even, last, first)
    outer_ref[...] = jnp.where(even, first, last)


def pad_copies(pad, own_ref, zlo_ref, zhi_ref, inner_ref, outer_ref):
    return [
        (own_ref, pad.at[1:9, 32:160]),
        (zlo_ref, pad.at[1:9, 0:32]),
        (zhi_ref, pad.at[1:9, 160:192]),
        (inner_ref, pad.at[(1 - own_core()) * (YL + 1)]),
        (outer_ref, pad.at[own_core() * (YL + 1)]),
    ]


def mix_kernel(recv_ref, weight_ref, table_ref, send_ref, spec_ref, rows_ref):
    spectrum = collect_spectrum(recv_ref, table_ref, rows_ref)
    spec_ref[...] = spectrum
    matrix = repeat_matrix()
    lane = lane_of((64, 128)) // 32
    real = jnp.zeros((64, 128), F32)
    imag = jnp.zeros((64, 128), F32)
    for k in range(KXL):
        wide = spread(spectrum, k, matrix)
        w_re = weight_ref[:, k * 2048 : k * 2048 + 1024].astype(F32)
        w_im = weight_ref[:, k * 2048 + 1024 : k * 2048 + 2048].astype(F32)
        s_re, s_im = wide[0:64], wide[64:128]
        real = jnp.where(lane == k, fold_tiles(s_re * w_re - s_im * w_im), real)
        imag = jnp.where(lane == k, fold_tiles(s_re * w_im + s_im * w_re), imag)
    modes = jnp.concatenate([real, imag], 0) * gain_lanes()
    send_ref[:, MODE_ROWS:] = jnp.zeros((GZ, 3 * MODE_ROWS, 128), BF16)
    send_ref[:, 0:MODE_ROWS] = z_inverse(modes, table_ref).astype(BF16).reshape(GZ, MODE_ROWS, 128)


def build_taps(kernel_ref, taps, flip):
    row = lax.broadcasted_iota(jnp.int32, (C, C), 0)
    eye = jnp.where(row == lane_of((C, C)), 1.0, 0.0).astype(BF16)
    tap = {}
    for dy in range(3):
        for dz in range(3):
            if flip:
                turned = dot_tn(kernel_ref[2 - dy, 2 - dz], eye)
                for dx in range(3):
                    tap[dx, dy, dz] = turned[(2 - dx) * C : (2 - dx) * C + C]
            else:
                whole = kernel_ref[dy, dz].astype(F32)
                for dx in range(3):
                    tap[dx, dy, dz] = whole[:, dx * C : dx * C + C]
    for dx in range(3):
        parts = []
        for dy in range(3):
            parts += [tap[dx, dy, dz] for dz in range(3)] + [jnp.zeros((C, 96), F32)]
        base = jnp.concatenate(parts + [jnp.zeros((C, 64), F32)], 1)
        for z in range(ZL):
            row = (dx * ZL + z) * C
            moved = pltpu.roll(base, z * C, 1) if z else base
            taps[row : row + C, :] = moved[:, 0:576].astype(BF16)


def conv_kernel(
    flip, own_ref, zlo_ref, zhi_ref, inner_ref, outer_ref, kernel_hbm, bias_hbm, out_ref,
    pad, taps, buffer, kernel_ref, bias_ref, in_sems, out_sems,
):
    fetched = begin(
        [(kernel_hbm, kernel_ref), (bias_hbm, bias_ref)]
        + pad_copies(pad, own_ref, zlo_ref, zhi_ref, inner_ref, outer_ref),
        in_sems,
    )
    finish(fetched[0:2])
    padded = fetched[2:]
    build_taps(kernel_ref, taps, flip)
    if not flip:
        row = lax.broadcasted_iota(jnp.int32, (128, C), 0) & 31
        picked = jnp.where(row == lane_of((128, C)), bias_ref[...], 0.0)
        bias = jnp.sum(picked, axis=1, keepdims=True)
    finish(padded)
    copies = []
    for y in range(YL):
        wide = dot(taps[...], pad[y : y + 3].reshape(576, NX))
        total = wide[128:256] + shift_right(wide[0:128]) + shift_left(wide[256:384])
        buffer[y] = (total if flip else total + bias).astype(BF16)
        if y % 4 == 3:
            half = slice(y - 3, y + 1)
            copies += begin([(buffer.at[half], out_ref.at[half])], out_sems.at[y // 4 : y // 4 + 1])
    finish(copies)


def slope_kernel(
    recv_ref, local_ref, cot_ref, own_ref, zlo_ref, zhi_ref, inner_ref, outer_ref, txi_hbm, tx_hbm,
    slope_ref, front_ref, back_ref, first_ref, last_ref, send_ref,
    recv, local, cot, pad, txi, tx, field_ref, slopes, sums_ref, in_sems, out_sems,
):
    fetched = begin(
        [(recv_ref, recv), (txi_hbm, txi), (tx_hbm, tx), (local_ref, local), (cot_ref, cot)]
        + pad_copies(pad, own_ref, zlo_ref, zhi_ref, inner_ref, outer_ref),
        in_sems,
    )
    fetched[0].wait()
    place_fields(recv, field_ref)
    finish(fetched[1:5])
    root = math.sqrt(2.0 / math.pi)
    lines = []
    for y in range(YL):
        pre = x_inverse(field_ref[y * 64 : y * 64 + 64], txi[...]) + local[y].astype(F32)
        square = pre * pre
        bent = jnp.tanh(root * pre * (1.0 + 0.044715 * square))
        rate = 0.5 * (1.0 + bent) + 0.5 * root * pre * (1.0 - bent * bent) * (
            1.0 + 3.0 * 0.044715 * square
        )
        slope = (cot[y].astype(F32) * rate).astype(BF16)
        slopes[y] = slope
        lines.append(dot_nt(tx[...], slope))
    copies = begin(
        face_copies(slopes, front_ref, back_ref, first_ref, last_ref) + [(slopes, slope_ref)], out_sems
    )
    pack_lines(lines, send_ref)
    finish(fetched[5:])
    bias = jnp.zeros((128, 1), F32)
    for start in range(0, YL, 4):
        left, right = ([], []), ([], [])
        for y in range(start, start + 4):
            slope = slopes[y]
            wide = slope.astype(F32)
            bias = bias + jnp.sum(wide, axis=1, keepdims=True)
            three = (shift_left(wide).astype(BF16), slope, shift_right(wide).astype(BF16))
            for half in range(2):
                left[half].append(jnp.concatenate([v[half * 64 : half * 64 + 64] for v in three], 0))
                right[half].append(pad[y : y + 3, half * 64 : half * 64 + 128].reshape(384, NX))
        for half in range(2):
            part = dot_nt(jnp.concatenate(left[half], 1), jnp.concatenate(right[half], 1))
            sums_ref[half] = part if start == 0 else sums_ref[half] + part
    bias32 = bias[0:32] + bias[32:64] + bias[64:96] + bias[96:128]
    pieces = []
    for dx in range(3):
        for dy in range(3):
            total = jnp.zeros((C, 96), F32)
            for z in range(ZL):
                row = (dx * 2 + z % 2) * C
                col = dy * 128 + z % 2 * C
                total = total + sums_ref[z // 2, row : row + C, col : col + 96]
            pieces += [total[:, dz * C : dz * C + C] for dz in range(3)]
    pieces.append(jnp.broadcast_to(bias32, (C, C)))
    for g in range(GY):
        if g < 7:
            rows = jnp.concatenate(pieces[4 * g : 4 * g + 4], 1)
        else:
            rows = jnp.zeros((C, 128), F32)
        high, low = split(rows)
        send_ref[g, LINE_ROWS : LINE_ROWS + GRAD_ROWS] = high
        send_ref[g, LINE_ROWS + GRAD_ROWS : LINE_ROWS + 2 * GRAD_ROWS] = low
    finish(copies)


def adjoint_kernel(recv_ref, weight_ref, table_ref, send_ref, spec_ref, rows_ref):
    spectrum = collect_spectrum(recv_ref, table_ref, rows_ref)
    spec_ref[...] = spectrum
    row = lax.broadcasted_iota(jnp.int32, (1024, 128), 0) // 32
    lane = lane_of((1024, 128))
    gather = []
    for k in range(KXL):
        w_re = weight_ref[:, k * 2048 : k * 2048 + 1024].astype(F32)
        w_im = weight_ref[:, k * 2048 + 1024 : k * 2048 + 2048].astype(F32)
        own = spectrum[:, k * 32 : k * 32 + 32]
        four = jnp.concatenate([own] * 4, 1)
        wide = jnp.concatenate([four] * 8, 1)
        b_re, b_im = wide[0:64], wide[64:128]
        both = jnp.concatenate([b_re * w_re + b_im * w_im, b_im * w_re - b_re * w_im], 0)
        matrix = jnp.where(row + k * 32 == lane, 1.0, 0.0).astype(BF16)
        high, low = split(both)
        gather.append(dot(high, matrix) + dot(low, matrix))
    modes = (gather[0] + gather[1] + gather[2] + gather[3]) * gain_lanes()
    send_ref[:, MODE_ROWS:] = jnp.zeros((GZ, 3 * MODE_ROWS, 128), BF16)
    block = z_inverse(modes, table_ref).astype(BF16)
    send_ref[:, 0:MODE_ROWS] = block.reshape(GZ, MODE_ROWS, 128)
    total = jnp.sum(recv_ref[:, MODE_ROWS : MODE_ROWS + TAIL_ROWS].astype(F32), axis=0)
    total = total + pltpu.roll(total, TAIL_ROWS - 2, 0)
    high = total.astype(BF16).astype(F32)
    part = lax.broadcasted_iota(jnp.int32, (TAIL_ROWS, 128), 0)
    low = jnp.where(part < 4, pltpu.roll(total - high, 2, 0), 0.0)
    tail = jnp.where(part < 2, high, low).astype(BF16)
    send_ref[:, MODE_ROWS : MODE_ROWS + TAIL_ROWS] = jnp.broadcast_to(tail[None], (GZ, TAIL_ROWS, 128))


def outer_kernel(spec_ref, back_ref, out_hbm, out_ref, sems):
    copies = []
    matrix = repeat_matrix()
    gain = gain_lanes()
    spectrum = spec_ref[...]
    back = back_ref[...] * gain
    for k in range(KXL):
        wide = spread(spectrum, k, matrix)
        s_re, s_im = wide[0:64], wide[64:128]
        own = back[:, k * 32 : k * 32 + 32]
        four = jnp.concatenate([own] * 4, 1)
        tiled = jnp.concatenate([four] * 8, 1)
        b_re, b_im = tiled[0:64], tiled[64:128]
        out_ref[:, k * 2048 : k * 2048 + 1024] = s_re * b_re + s_im * b_im
        out_ref[:, k * 2048 + 1024 : k * 2048 + 2048] = s_re * b_im - s_im * b_re
        part = slice(k * 2048, k * 2048 + 2048)
        copies += begin([(out_ref.at[:, part], out_hbm.at[:, part])], sems.at[k : k + 1])
    finish(copies)


def final_kernel(
    recv_ref, conv_ref, txi_hbm, grad_ref, kernel_ref, bias_ref,
    recv, conv, txi, field_ref, grads, in_sems, out_sems,
):
    fetched = begin([(recv_ref, recv), (txi_hbm, txi), (conv_ref, conv)], in_sems)
    fetched[0].wait()
    place_fields(recv, field_ref)
    finish(fetched[1:])
    copies = []
    for y in range(YL):
        back = x_inverse(field_ref[y * 64 : y * 64 + 64], txi[...])
        grads[y] = (back + conv[y].astype(F32)).astype(BF16)
        if y % 4 == 3:
            half = slice(y - 3, y + 1)
            copies += begin([(grads.at[half], grad_ref.at[half])], out_sems.at[y // 4 : y // 4 + 1])
    piece = []
    for g in range(7):
        high = recv[g, LINE_ROWS : LINE_ROWS + GRAD_ROWS].astype(F32)
        low = recv[g, LINE_ROWS + GRAD_ROWS : LINE_ROWS + 2 * GRAD_ROWS].astype(F32)
        rows = SCALE * (high + low)
        piece += [rows[:, j * C : j * C + C] for j in range(4)]
    for dy in range(3):
        for dz in range(3):
            kernel_ref[dy, dz] = jnp.concatenate([piece[dx * 9 + dy * 3 + dz] for dx in range(3)], 1)
    row = lax.broadcasted_iota(jnp.int32, (C, C), 0)
    bias_ref[...] = jnp.sum(jnp.where(row == lane_of((C, C)), piece[27], 0.0), axis=0, keepdims=True)
    finish(copies)


AUTO, HBM = pl.BlockSpec(), pl.BlockSpec(memory_space=pltpu.HBM)


def vmem(dims, kind):
    return pltpu.VMEM(dims, kind)


def sems(count):
    return pltpu.SemaphoreType.DMA((count,))


def shape(dims, kind):
    return jax.ShapeDtypeStruct(dims, kind)


def call(body, ins, outs, scratch, room, *operands):
    return pl.pallas_call(
        body,
        in_specs=ins,
        out_specs=[spec for spec, _ in outs],
        out_shape=[kind for _, kind in outs],
        scratch_shapes=scratch,
        compiler_params=pltpu.CompilerParams(vmem_limit_bytes=room),
    )(*operands)


def exchange(blocks, axis):
    return lax.all_to_all(blocks, axis, 0, 0, tiled=True)


FIELD = shape((YL, 128, NX), BF16)
SIDE = shape((YL, 32, NX), BF16)
FACE = shape((128, NX), BF16)
EDGE = shape((192, NX), BF16)
PAD = vmem((YL + 2, 192, NX), BF16)


def after(value, *others):
    return lax.optimization_barrier((value, *others))[0]


def z_halos(front, back):
    zlo = lax.ppermute(back, "gz", [(i, i + 1) for i in range(GZ - 1)])
    zhi = lax.ppermute(front, "gz", [(i + 1, i) for i in range(GZ - 1)])
    return zlo, zhi


def y_edges(first, last, zlo, zhi):
    return call(edges_kernel, [AUTO] * 4, [(AUTO, EDGE)] * 2, [], SMALL, first, last, zlo, zhi)


def y_halos(inner, outer):
    ahead = [(i, i + 1) for i in range(1, GY - 1, 2)]
    behind = [(i, i - 1) for i in range(2, GY, 2)]
    outer = lax.ppermute(outer, "gy", ahead + behind)
    inner = lax.ppermute(inner, "gy", [(i, i ^ 1) for i in range(GY)])
    return inner, outer


def conv(flip, own, halo, kernel, bias):
    return call(
        functools.partial(conv_kernel, flip),
        [HBM] * 7,
        [(HBM, FIELD)],
        [
            PAD, vmem((384, 576), BF16), vmem((YL, 128, NX), BF16),
            vmem((3, 3, C, 3 * C), BF16), vmem((1, C), F32), sems(7), sems(2),
        ],
        LARGE,
        own, *halo, kernel, bias,
    )[0]


def on_device(features, cotangent, spectral_weight, kernel_weight, channel_bias):
    own = features.reshape(YL, 128, NX)
    cot = cotangent.reshape(YL, 128, NX)
    weight = spectral_weight.reshape(64, 8192)
    bias = channel_bias.reshape(1, C)
    tx = jnp.asarray(x_forward_table())
    txi = jnp.asarray(x_inverse_table())
    table = jnp.asarray(joint_table())
    faces_out = [(HBM, SIDE)] * 2 + [(HBM, FACE)] * 2
    spectrum_out = (AUTO, shape((128, 128), F32))

    def lines_out(rows):
        return AUTO, shape((GY, rows, 128), BF16)

    def modes_out(rows):
        return AUTO, shape((GZ, rows, 128), BF16)

    both_rows = LINE_ROWS + 2 * GRAD_ROWS
    tail_rows = MODE_ROWS + TAIL_ROWS
    send, front, back, first, last = call(
        analyse_kernel,
        [HBM] * 2,
        [lines_out(2 * LINE_ROWS)] + faces_out,
        [vmem((YL, 128, NX), BF16), vmem((64, NX), BF16), sems(2), sems(4)],
        LARGE,
        own, tx,
    )
    recv = exchange(send, "gy")

    zlo, zhi = z_halos(front, back)
    (send,) = call(y_kernel, [AUTO] * 2, [modes_out(MODE_ROWS)], [], SMALL, recv, table)
    recv = exchange(send, "gz")
    send, spectrum = call(
        mix_kernel,
        [AUTO] * 3,
        [modes_out(4 * MODE_ROWS), spectrum_out],
        [vmem((256, 128), F32)],
        SMALL,
        recv, weight, table,
    )
    halo = (zlo, zhi, *y_halos(*y_edges(after(first, send), last, zlo, zhi)))
    recv = exchange(send, "gz")
    recv, inner = lax.optimization_barrier((recv, halo[2]))
    halo = (zlo, zhi, inner, halo[3])
    (send,) = call(spread_kernel, [AUTO] * 2, [lines_out(LINE_ROWS)], [], SMALL, recv, table)
    local = conv(False, after(own, send), halo, kernel_weight, bias)
    recv = exchange(send, "gy")
    slope, front, back, first, last, send = call(
        slope_kernel,
        [HBM] * 10,
        [(HBM, FIELD)] + faces_out + [lines_out(both_rows)],
        [
            vmem((GY, LINE_ROWS, 128), BF16), vmem((YL, 128, NX), BF16), vmem((YL, 128, NX), BF16), PAD,
            vmem((192, NX), BF16), vmem((64, NX), BF16), vmem((512, 128), F32), vmem((YL, 128, NX), BF16),
            vmem((2, 192, 384), F32), sems(10), sems(5),
        ],
        LARGE,
        recv, local, cot, own, *halo, txi, tx,
    )
    recv = exchange(send, "gy")

    zlo, zhi = z_halos(front, back)
    (send,) = call(
        y_back_kernel,
        [AUTO] * 2,
        [modes_out(tail_rows)],
        [vmem((GRAD_ROWS, 128), F32), vmem((GZ * TAIL_ROWS, 128), F32)],
        SMALL,
        recv, table,
    )
    recv = exchange(send, "gz")
    send, back = call(
        adjoint_kernel,
        [AUTO] * 3,
        [modes_out(4 * MODE_ROWS), spectrum_out],
        [vmem((256, 128), F32)],
        SMALL,
        recv, weight, table,
    )
    halo = (zlo, zhi, *y_halos(*y_edges(after(first, send), last, zlo, zhi)))
    recv = exchange(send, "gz")
    (grad_spectral,) = call(
        outer_kernel,
        [AUTO] * 2,
        [(HBM, shape((64, 8192), F32))],
        [vmem((64, 8192), F32), sems(KXL)],
        MEDIUM,
        after(spectrum, send), back,
    )
    recv, grad_spectral, *halo = lax.optimization_barrier((recv, grad_spectral, *halo))
    (send,) = call(
        spread_back_kernel,
        [AUTO] * 2,
        [lines_out(both_rows)],
        [vmem((GZ * TAIL_ROWS, 128), F32), vmem((2 * GRAD_ROWS, 128), F32)],
        SMALL,
        recv, table,
    )
    recv = exchange(send, "gy")
    conv_field = conv(True, after(slope, send), halo, kernel_weight, bias)
    grad_field, grad_kernel, grad_bias = call(
        final_kernel,
        [HBM] * 3,
        [(HBM, FIELD), (AUTO, shape((3, 3, C, 3 * C), F32)), (AUTO, shape((1, C), F32))],
        [
            vmem((GY, both_rows, 128), BF16), vmem((YL, 128, NX), BF16), vmem((192, NX), BF16),
            vmem((512, 128), F32), vmem((YL, 128, NX), BF16), sems(3), sems(2),
        ],
        MEDIUM,
        recv, conv_field, txi,
    )
    return (
        grad_field.reshape(features.shape),
        grad_spectral.reshape(spectral_weight.shape),
        grad_kernel,
        grad_bias.reshape(C),
    )


def solution(mesh):
    return jax.shard_map(
        on_device,
        mesh=mesh,
        in_specs=(
            P("gy", "gz", None, None),
            P("gy", "gz", None, None),
            P("gz", None, "gy"),
            P(),
            P(),
        ),
        out_specs=(P("gy", "gz", None, None), P("gz", None, "gy"), P(), P()),
        check_vma=False,
    )
```
